512 devices in a mesh: pp: 32 (over x_hi, z), ep: 16 (over x_lo, y, core).
Axes of the slice: x: 4 (x_hi: 2, x_lo: 2; x = x_hi * 2 + x_lo), y: 4, z: 16, core: 2. Of those that a mesh axis runs over, the one named last changes fastest.
Arguments:
- section_out: bfloat16 [32768, 3584], P(('pp', 'ep')), may hold values from -6 to 6
- routes_fwd: int32 [32768, 1], P(('pp', 'ep')), may hold values from 0 to 1; in each aligned block of 64 rows (0 to 63, 64 to 127, ...) at most 32 rows name the same one
- gates_fwd: float32 [32768, 1], P(('pp', 'ep')), may hold values from 0.1 to 1
- cot_next: bfloat16 [32768, 3584], P(('pp', 'ep')), may hold values from -6 to 6
- routes_bwd: int32 [32768, 1], P(('pp', 'ep')), may hold values from 0 to 1; in each aligned block of 64 rows (0 to 63, 64 to 127, ...) at most 32 rows name the same one
- gates_bwd: float32 [32768, 1], P(('pp', 'ep')), may hold values from 0.1 to 1
- norm_gain: float32 [32, 3584], P('pp'), may hold values from 0.1 to 1.9
- saved_gate: bfloat16 [32, 512, 2048], P('pp', None, 'ep'), may hold values from -6 to 6
- saved_up: bfloat16 [32, 512, 2048], P('pp', None, 'ep'), may hold values from -6 to 6
- w_gate: bfloat16 [32, 3584, 2048], P('pp', None, 'ep'), may hold values from -0.09375 to 0.09375
- w_up: bfloat16 [32, 3584, 2048], P('pp', None, 'ep'), may hold values from -0.09375 to 0.09375
- w_down: bfloat16 [32, 2048, 3584], P('pp', 'ep'), may hold values from -0.1875 to 0.1875
Outputs:
- section_result: bfloat16 [32768, 3584], P(('pp', 'ep'))
- input_grad: bfloat16 [32768, 3584], P(('pp', 'ep'))
The draws below stay inside these ranges and needn't reach their ends.
Inputs may be any that keep to these rules, and one draw needn't show every extreme that they name: `routes_fwd`: in the rows of one device each expert is named exactly 32 times. `routes_bwd`: as for routes_fwd.
All inputs are finite; a program needn't handle non-finite values.
Results may differ from the reference program's by a relative error of at most 0.0064.
Values may be sent and summed in bfloat16 or wider, within the bound.
A program may use at most 64 MiB of HBM per device.

```python
import math
import jax
import jax.numpy as jnp
import numpy as np
from jax import lax

D = 3584
F = 1024
EXPERTS = 2
TOPK = 1
HALF = 64
GROUP = 8
F_DEV = 128
CAP = 32
SLOTS = 512
ROWS = 32768
N_PP = 32
N_EP = 16


def block_levels(own_key, extent, pieces, smallest, largest):
    level, own = 1.0, jax.random.fold_in(own_key, 6)
    for axis_at, shards_of in pieces:
        draws = jnp.exp(jax.random.uniform(jax.random.fold_in(own, axis_at), (shards_of,), jnp.float32, smallest / len(pieces), largest / len(pieces)))
        level = level * jnp.repeat(draws, extent[axis_at] // shards_of).reshape([-1 if axis == axis_at else 1 for axis in range(len(extent))])
    return level


def shared_out(stream_key, own, number, rows, amount, top, most, lean):
    ranking = jax.random.permutation(stream_key, amount)
    crowded, common = shares(amount, rows * top, most, lean, True), shares(amount, rows * top, most, lean, False)
    places = jnp.arange(amount)

    def named(tallies, turn):
        used = int((tallies > 0).sum())
        fixed = max(1, used // 4)
        passed = fixed + (places - fixed + turn * (used - fixed)) % max(1, amount - fixed)
        return jnp.zeros((amount,), jnp.int32).at[ranking[jnp.where(places < fixed, places, passed)]].set(jnp.asarray(tallies, jnp.int32))

    tallies = jnp.where(number % 4 == 0, named(crowded, number // 4), named(common, number - number // 4 - 1))
    mixed = jax.random.permutation(jax.random.fold_in(own, 3), amount)
    source_of, taker = mixed[0:amount // 2 * 2:2], mixed[1:amount // 2 * 2:2]
    room = jnp.minimum(tallies[source_of] - 1, most - tallies[taker]) // 2
    room = jnp.where((source_of == ranking[0]) | (taker == ranking[0]) | (tallies[taker] == 0), 0, jnp.maximum(room, 0))
    passed = jax.random.randint(jax.random.fold_in(own, 4), (amount // 2,), 0, 1 << 20) % (room + 1)
    tallies = tallies.at[source_of].add(-passed).at[taker].add(passed)
    labels = jnp.searchsorted(jnp.cumsum(tallies), jnp.arange(rows * top), side="right").astype(jnp.int32)
    listing = labels.reshape(top, rows).T
    listing = listing[jax.random.permutation(jax.random.fold_in(own, 1), rows)]
    turn = jax.random.randint(jax.random.fold_in(own, 2), (rows, 1), 0, top)
    return jnp.take_along_axis(listing, (jnp.arange(top)[None, :] + turn) % top, axis=1)


def shares(amount, total, limit, lean, full):
    portions = [(1 << 20) // math.isqrt(standing ** lean) + 1 for standing in range(1, amount + 1)]
    largest = limit if full else min(limit, max(-(-total // amount), total * portions[0] // sum(portions)))
    least = 1 if total - largest >= amount - 1 else 0
    given, spare = [largest] + [least] * (amount - 1), total - largest - least * (amount - 1)
    while spare > 0:
        free = [i for i in range(1, amount) if given[i] < largest] or [i for i in range(1, amount) if given[i] < limit]
        pool, budget = sum([portions[i] for i in free]), spare
        for i in free:
            addition = min(limit - given[i], max(1, budget * portions[i] // pool), spare)
            given[i] = given[i] + addition
            spare = spare - addition
    return np.array(given)


def normal_values(stream_key, shape, spread, most, cuts=(), kind=jnp.bfloat16):
    entries = spread * jax.random.normal(stream_key, shape, jnp.float32)
    if cuts:
        entries = entries * block_levels(stream_key, shape, cuts, -0.22, 0.18)
    return jnp.clip(entries, -most, most).astype(kind)


def setup_inputs(seed: int = 0) -> dict:
    seeds = jax.random.split(jax.random.key(seed), 13)
    section_out = normal_values(seeds[0], (ROWS, D), 1.0, 6.0, ((0, 512),))
    routes_fwd_keys = jax.random.split(jax.random.fold_in(seeds[1], 1), ROWS // HALF)
    routes_fwd_turns = jax.random.permutation(jax.random.fold_in(seeds[1], 3), ROWS // HALF)
    routes_fwd = jax.vmap(lambda own, number: shared_out(jax.random.fold_in(seeds[1], 2), own, number, HALF, EXPERTS, TOPK, CAP, 0))(routes_fwd_keys, routes_fwd_turns).reshape((ROWS, TOPK))
    gates_fwd = jnp.clip(jnp.exp(math.log(1.0) - 2.3025851 * jax.random.uniform(seeds[2], (ROWS, TOPK), jnp.float32) ** block_levels(seeds[2], (ROWS, TOPK), ((0, 512),), -0.2, 0.2)), 0.1, 1.0)
    cot_next = normal_values(seeds[3], (ROWS, D), 1.0, 6.0, ((0, 512),))
    routes_bwd_keys = jax.random.split(jax.random.fold_in(seeds[4], 1), ROWS // HALF)
    routes_bwd_turns = jax.random.permutation(jax.random.fold_in(seeds[4], 3), ROWS // HALF)
    routes_bwd = jax.vmap(lambda own, number: shared_out(jax.random.fold_in(seeds[4], 2), own, number, HALF, EXPERTS, TOPK, CAP, 0))(routes_bwd_keys, routes_bwd_turns).reshape((ROWS, TOPK))
    gates_bwd = jnp.clip(jnp.exp(math.log(1.0) - 2.3025851 * jax.random.uniform(seeds[5], (ROWS, TOPK), jnp.float32) ** block_levels(seeds[5], (ROWS, TOPK), ((0, 512),), -0.2, 0.2)), 0.1, 1.0)
    norm_gain = jnp.clip(1.0 + 0.18 * jax.random.normal(seeds[6], (N_PP, D), jnp.float32), 0.1, 1.9)
    saved_gate = normal_values(seeds[7], (N_PP, SLOTS, EXPERTS * F), 1.0, 6.0, ((0, 32), (2, 16)))
    saved_up = normal_values(seeds[8], (N_PP, SLOTS, EXPERTS * F), 1.0, 6.0, ((0, 32), (2, 16)))
    w_gate = normal_values(seeds[9], (N_PP, D, EXPERTS * F), D ** -0.5, 0.09375, ((0, 32), (2, 16)))
    w_up = normal_values(seeds[10], (N_PP, D, EXPERTS * F), D ** -0.5, 0.09375, ((0, 32), (2, 16)))
    w_down = normal_values(seeds[11], (N_PP, EXPERTS * F, D), F ** -0.5, 0.1875, ((0, 32), (1, 16)))
    return dict(section_out=section_out, routes_fwd=routes_fwd, gates_fwd=gates_fwd, cot_next=cot_next, routes_bwd=routes_bwd, gates_bwd=gates_bwd, norm_gain=norm_gain, saved_gate=saved_gate, saved_up=saved_up, w_gate=w_gate, w_up=w_up, w_down=w_down)


EPS = 1e-06

def slot_places(routes, experts, capacity):
    flat = routes.reshape(-1).astype(jnp.int32)
    onehot = (flat[:, None] == jnp.arange(experts, dtype=jnp.int32)[None, :]).astype(jnp.int32)
    before = jnp.cumsum(onehot, axis=0) - onehot
    slot = lax.optimization_barrier(jnp.sum(before * onehot, axis=1)).astype(jnp.int32)
    return (flat * capacity + slot).astype(jnp.int32)

def normalize(values, gain):
    floats = values.astype(jnp.float32)
    scale = lax.rsqrt(lax.optimization_barrier(jnp.mean(floats * floats, axis=-1, keepdims=True)) + EPS)
    return (floats * scale * gain).astype(jnp.bfloat16)

def dispatch(rows, places, experts, capacity):
    buffer = jnp.zeros((experts * capacity, rows.shape[-1]), rows.dtype)
    buffer = buffer.at[places].set(rows)
    return buffer.reshape(experts, capacity, rows.shape[-1])

def contract_last(left, right):
    return lax.dot_general(left, right, (((1,), (1,)), ((), ())), preferred_element_type=jnp.float32)

def slice_forward(rows, gate_cols, up_cols, down_rows):
    gate_act = jnp.dot(rows, gate_cols, preferred_element_type=jnp.float32)
    up_act = jnp.dot(rows, up_cols, preferred_element_type=jnp.float32)
    inner = (gate_act * jax.nn.sigmoid(gate_act) * up_act).astype(jnp.bfloat16)
    return jnp.dot(inner, down_rows, preferred_element_type=jnp.float32).astype(jnp.bfloat16)

def slice_backward(scaled, gate_act, up_act, gate_cols, up_cols, down_rows):
    inner_grad = contract_last(scaled, down_rows)
    sigma = jax.nn.sigmoid(gate_act)
    gate_grad = (inner_grad * up_act * sigma * (1.0 + gate_act * (1.0 - sigma))).astype(jnp.bfloat16)
    up_grad = (inner_grad * gate_act * sigma).astype(jnp.bfloat16)
    total = contract_last(gate_grad, gate_cols) + contract_last(up_grad, up_cols)
    return total.astype(jnp.bfloat16)

def by_expert(buffers):
    return buffers.transpose(1, 0, 2, 3).reshape(EXPERTS, SLOTS, D)

def combine_back(partials, places):
    floats = partials.astype(jnp.float32).reshape(EXPERTS, GROUP, N_EP, CAP, D)
    summed = lax.optimization_barrier(jnp.sum(floats, axis=1))
    per_source = summed.transpose(1, 0, 2, 3).reshape(N_EP, EXPERTS * CAP, D)
    return jax.vmap(lambda back, where: back[where])(per_source, places)

def section_work(items):
    arrived, routes_a, gates_a, upstream, routes_b, gates_b, gain, held_gate, held_up, gate_weight, up_weight, down_weight = items
    places_a = jax.vmap(lambda routes: slot_places(routes, EXPERTS, CAP))(routes_a)
    places_b = jax.vmap(lambda routes: slot_places(routes, EXPERTS, CAP))(routes_b)
    hidden_a = normalize(arrived, gain)
    place_rows = jax.vmap(lambda rows, places: dispatch(rows, places, EXPERTS, CAP))
    buffer_a = by_expert(place_rows(jnp.repeat(hidden_a, TOPK, axis=1), places_a))
    grad_out = upstream.astype(jnp.float32)
    scaled = (gates_b[:, :, :, None] * grad_out[:, :, None, :]).astype(jnp.bfloat16)
    buffer_c = by_expert(place_rows(scaled.reshape(N_EP, HALF * TOPK, D), places_b))

    def one_device(device):
        expert = (device // GROUP).astype(jnp.int32)
        start = (device * F_DEV).astype(jnp.int32)
        gate_cols = lax.dynamic_slice_in_dim(gate_weight, start, F_DEV, 1)
        up_cols = lax.dynamic_slice_in_dim(up_weight, start, F_DEV, 1)
        down_rows = lax.dynamic_slice_in_dim(down_weight, start, F_DEV, 0)
        rows_a = lax.dynamic_index_in_dim(buffer_a, expert, 0, keepdims=False)
        rows_c = lax.dynamic_index_in_dim(buffer_c, expert, 0, keepdims=False)
        gate_act = lax.dynamic_slice_in_dim(held_gate, start, F_DEV, 1).astype(jnp.float32)
        up_act = lax.dynamic_slice_in_dim(held_up, start, F_DEV, 1).astype(jnp.float32)
        forward_part = slice_forward(rows_a, gate_cols, up_cols, down_rows)
        backward_part = slice_backward(rows_c, gate_act, up_act, gate_cols, up_cols, down_rows)
        return (forward_part, backward_part)
    parts_a, parts_b = lax.map(one_device, jnp.arange(N_EP, dtype=jnp.int32))
    picked_a = combine_back(parts_a, places_a).reshape(N_EP, HALF, TOPK, D)
    result = arrived.astype(jnp.float32) + lax.optimization_barrier(jnp.sum(picked_a * gates_a[:, :, :, None], axis=2))
    picked_b = combine_back(parts_b, places_b).reshape(N_EP, HALF, TOPK, D)
    grad_in = lax.optimization_barrier(jnp.sum(picked_b, axis=2))
    return (result.astype(jnp.bfloat16), grad_in.astype(jnp.bfloat16))

def reference(section_out, routes_fwd, gates_fwd, cot_next, routes_bwd, gates_bwd, norm_gain, saved_gate, saved_up, w_gate, w_up, w_down):
    blocks = (N_PP, N_EP, HALF)
    arrived = jnp.roll(section_out.reshape(blocks + (D,)), 1, axis=0)
    upstream = jnp.roll(cot_next.reshape(blocks + (D,)), -1, axis=0)
    items = (arrived, routes_fwd.reshape(blocks + (TOPK,)), gates_fwd.reshape(blocks + (TOPK,)), upstream, routes_bwd.reshape(blocks + (TOPK,)), gates_bwd.reshape(blocks + (TOPK,)), norm_gain, saved_gate, saved_up, w_gate, w_up, w_down)
    result, grad_in = lax.map(section_work, items)
    return (result.reshape(ROWS, D), grad_in.reshape(ROWS, D))
```

```python
import functools

import jax
import jax.numpy as jnp
from jax import lax
from jax.experimental import pallas as pl
from jax.experimental.pallas import tpu as pltpu
from jax.sharding import PartitionSpec as P

EXPERTS = 2
RING = 4
CORES = 2
EPS = 1e-06
CHUNKS = 7
START = 11
MESH = pl.DeviceIdType.MESH


def kernel(
    section_out,
    cot_next,
    routes_fwd,
    gates_fwd,
    routes_bwd,
    gates_bwd,
    norm_gain,
    saved_gate,
    saved_up,
    w_gate,
    w_up,
    w_down,
    result,
    grad_in,
    arr,
    disp,
    rows,
    gate_up,
    down,
    held_gate,
    held_up,
    pick,
    unpick,
    factor,
    row_gate,
    gate_out,
    act,
    squares,
    inner,
    back_act,
    back_inner,
    part,
    far_send,
    far_recv,
    near_send,
    near_recv,
    home_send,
    home,
    out_buf,
    load_sem,
    core_send,
    core_recv,
    pp_send,
    pp_recv,
    x_send,
    x_recv,
    y_send,
    y_recv,
    far_send_sem,
    far_recv_sem,
    near_send_sem,
    near_recv_sem,
    home_send_sem,
    home_recv_sem,
    gate_send_sem,
    gate_recv_sem,
    out_sem,
):
    count = section_out.shape[0]
    width = section_out.shape[1]
    cap = count // EXPERTS
    unit = w_gate.shape[2]
    units = unit * CORES
    cw = width // CHUNKS
    total = EXPERTS * RING * cap
    steps = 2 * CHUNKS
    f32, bf16 = jnp.float32, jnp.bfloat16

    me_pp = lax.axis_index("pp")
    me = lax.axis_index("ep")
    n_pp = lax.axis_size("pp")
    plane = me // (RING * CORES)
    other = 1 - plane
    y = (me // CORES) % RING
    core = me % CORES

    def in_ring(at):
        return {"ep": plane * (RING * CORES) + at * CORES + core}

    y_up = lax.rem(y + 1, RING)
    y_far = lax.rem(y + 2, RING)
    y_down = lax.rem(y + 3, RING)
    up = in_ring(y_up)
    dn = in_ring(y_down)
    across = {"ep": other * (RING * CORES) + y * CORES + core}
    twin = {"ep": plane * (RING * CORES) + y * CORES + (1 - core)}
    after = {"pp": lax.rem(me_pp + 1, n_pp)}
    before = {"pp": lax.rem(me_pp + n_pp - 1, n_pp)}

    own_lane = pl.multiple_of(core * unit, unit)

    def load(src, dst, at):
        return pltpu.make_async_copy(src, dst, load_sem.at[at])

    loads = [
        load(w_gate.at[0], gate_up.at[:, pl.ds(own_lane, unit)], 0),
        load(w_up.at[0], gate_up.at[:, pl.ds(pl.multiple_of(units + core * unit, unit), unit)], 1),
        load(w_down.at[0], down.at[pl.ds(own_lane, unit)], 2),
        load(saved_gate.at[:, core], held_gate.at[:, :, pl.ds(own_lane, unit)], 3),
        load(saved_up.at[:, core], held_up.at[:, :, pl.ds(own_lane, unit)], 4),
    ]
    for one in loads:
        one.start()

    barrier = pltpu.get_barrier_semaphore()
    for neighbour in (after, before, up, dn, across, twin):
        pl.semaphore_signal(barrier, inc=1, device_id=neighbour, device_id_type=MESH)
    pl.semaphore_wait(barrier, 6)

    def remote(src, dst, send, recv, to):
        return pltpu.make_async_remote_copy(
            src_ref=src, dst_ref=dst, send_sem=send, recv_sem=recv, device_id=to, device_id_type=MESH
        )

    def pp_copy(t, src, j, to):
        return remote(
            src.at[:, pl.ds(pl.multiple_of(j * cw, cw), cw)], arr.at[t], pp_send, pp_recv.at[t], to
        )

    def start_pp(j, carry):
        pp_copy(j, section_out, j, after).start()
        pp_copy(CHUNKS + j, cot_next, j, before).start()
        return carry

    lax.fori_loop(0, CHUNKS, start_pp, 0)

    def shared(src, dst, at):
        return remote(src, dst, core_send.at[at], core_recv.at[at], twin)

    shares = [
        shared(w_gate.at[0], gate_up.at[:, pl.ds(own_lane, unit)], 0),
        shared(w_up.at[0], gate_up.at[:, pl.ds(pl.multiple_of(units + core * unit, unit), unit)], 1),
        shared(w_down.at[0], down.at[pl.ds(own_lane, unit)], 2),
        shared(saved_gate.at[:, 1 - core], held_gate.at[:, :, pl.ds(own_lane, unit)], 3),
        shared(saved_up.at[:, 1 - core], held_up.at[:, :, pl.ds(own_lane, unit)], 4),
    ]
    for one in shares:
        one.start()

    first = lax.broadcasted_iota(jnp.int32, (count, count), 0)
    second = lax.broadcasted_iota(jnp.int32, (count, count), 1)
    diagonal = first == second
    ones = jnp.ones((count, count), bf16)

    def places(routes, m):
        along = jnp.broadcast_to(routes[...].astype(f32), (count, count))
        down_rows = jnp.dot(jnp.where(diagonal, along, 0.0).astype(bf16), ones, preferred_element_type=f32)
        same = along == down_rows
        earlier = jnp.where(same & (first < second), 1.0, 0.0)
        place_along = along * cap + jnp.sum(earlier, axis=0, keepdims=True)
        chosen = place_along == first.astype(f32)
        pick[m] = jnp.where(chosen, 1.0, 0.0).astype(bf16)
        earlier = jnp.where(same & (second < first), 1.0, 0.0)
        place_down = down_rows * cap + jnp.sum(earlier, axis=1, keepdims=True)
        unpick[m] = jnp.where(place_down == second.astype(f32), 1.0, 0.0).astype(bf16)
        return chosen

    chosen = places(routes_fwd, 0)
    slot_gate = jnp.sum(jnp.where(chosen, jnp.broadcast_to(gates_fwd[...], (count, count)), 0.0), axis=1, keepdims=True)
    gate_out[...] = jnp.broadcast_to(slot_gate, (count, 128)).reshape(EXPERTS, cap, 128)
    row_gate[0, plane] = gate_out[plane]
    gate_copy = remote(gate_out.at[other], row_gate.at[0, plane], gate_send_sem, gate_recv_sem, across)
    gate_copy.start()
    row_gate[1] = jnp.ones((EXPERTS, cap, 128), f32)
    factor[0] = jnp.ones((count, 128), f32)
    chosen = places(routes_bwd, 1)
    slot_gate = jnp.sum(jnp.where(chosen, jnp.broadcast_to(gates_bwd[...], (count, count)), 0.0), axis=1, keepdims=True)
    factor[1] = jnp.broadcast_to(slot_gate, (count, 128))
    squares[...] = jnp.zeros_like(squares)
    act[...] = jnp.zeros_like(act)
    back_act[...] = jnp.zeros_like(back_act)

    def columns(j):
        return pl.ds(pl.multiple_of(j * cw, cw), cw)

    def cross(t):
        return remote(disp.at[t, other], rows.at[t, plane, y], x_send, x_recv.at[t], across)

    def crossed(t):
        return remote(disp.at[t, other], rows.at[t, other, y], x_send, x_recv.at[t], across)

    def ring_copy(t, side, at, to, sem):
        return remote(rows.at[t, side, at], rows.at[t, side, at], y_send.at[sem], y_recv.at[t, sem], to)

    def dispatch(t):
        m = t // CHUNKS
        pp_copy(t, section_out, 0, after).wait_recv()
        moved = jnp.dot(pick[m], arr[t], preferred_element_type=f32) * factor[m][:, 0:1]
        disp[t] = moved.astype(bf16).reshape(EXPERTS, cap, cw)
        cross(t).start()
        rows[t, plane, y] = disp[t, plane]
        ring_copy(t, plane, y, up, plane).start()
        ring_copy(t, plane, y, dn, 2 + plane).start()

    def spread(t):
        crossed(t).wait_recv()
        ring_copy(t, other, y, up, other).start()
        ring_copy(t, other, y, dn, 2 + other).start()

    def forward(t):
        ring_copy(t, 0, y_down, up, 0).wait_recv()
        ring_copy(t, 0, y_down, up, 4).start()
        ring_copy(t, 1, y_up, dn, 3).wait_recv()
        ring_copy(t, 1, y_up, dn, 5).start()

    def gathered(t):
        ring_copy(t, 1, y_down, up, 1).wait_recv()
        ring_copy(t, 0, y_up, dn, 2).wait_recv()
        ring_copy(t, 0, y_far, up, 4).wait_recv()
        ring_copy(t, 1, y_far, dn, 5).wait_recv()

    def multiply_fwd(t):
        @pl.when(t == 0)
        def _():
            for at in (0, 1):
                loads[at].wait()
                shares[at].wait_recv()

        floats = rows[t].reshape(total, cw).astype(f32)
        squared = floats * floats
        lanes = squared[:, 0:128]
        for k in range(1, cw // 128):
            lanes = lanes + squared[:, k * 128 : (k + 1) * 128]
        squares[...] += lanes
        left = (floats * norm_gain[:, columns(t)]).astype(bf16)
        act[...] += jnp.dot(left, gate_up[columns(t), :], preferred_element_type=f32)

        @pl.when(t == CHUNKS - 1)
        def _():
            mean = jnp.sum(squares[...], axis=1, keepdims=True) * (1.0 / width)
            scale = lax.rsqrt(mean + EPS)
            gate_act = act[:, 0:units] * scale
            up_act = act[:, units : 2 * units] * scale
            inner[...] = (gate_act * jax.nn.sigmoid(gate_act) * up_act).astype(bf16)

    def multiply_bwd(t):
        j = t - CHUNKS

        @pl.when(j == 0)
        def _():
            for at in (2, 3, 4):
                loads[at].wait()
                shares[at].wait_recv()

        back_act[...] += lax.dot_general(
            rows[t].reshape(total, cw), down[:, columns(j)], (((1,), (1,)), ((), ())), preferred_element_type=f32
        )

        @pl.when(j == CHUNKS - 1)
        def _():
            inner_grad = back_act[...]
            gate_act = held_gate[...].reshape(total, units).astype(f32)
            up_act = held_up[...].reshape(total, units).astype(f32)
            sigma = jax.nn.sigmoid(gate_act)
            gate_grad = inner_grad * up_act * sigma * (1.0 + gate_act * (1.0 - sigma))
            back_inner[:, 0:units] = gate_grad.astype(bf16)
            back_inner[:, units : 2 * units] = (inner_grad * gate_act * sigma).astype(bf16)

    def far_copy(u, way, to):
        return remote(far_send.at[u, way], far_recv.at[u, way], far_send_sem.at[way], far_recv_sem.at[u, way], to)

    def near_copy(u, way, to):
        return remote(near_send.at[u, way], near_recv.at[u, way], near_send_sem.at[way], near_recv_sem.at[u, way], to)

    def produce(u):
        @pl.when(u < CHUNKS)
        def _():
            value = jnp.dot(inner[...], down[:, columns(u)], preferred_element_type=f32)
            part[u] = value.reshape(EXPERTS, RING, cap, cw)

        @pl.when(u >= CHUNKS)
        def _():
            value = lax.dot_general(
                back_inner[...],
                gate_up[columns(u - CHUNKS), :],
                (((1,), (1,)), ((), ())),
                preferred_element_type=f32,
            )
            part[u] = value.reshape(EXPERTS, RING, cap, cw)

        far_send[u, 0] = part[u, 0, y_far].astype(bf16)
        far_send[u, 1] = part[u, 1, y_far].astype(bf16)
        far_copy(u, 0, up).start()
        far_copy(u, 1, dn).start()

    def add_far(u):
        near_send[u, 0, 1] = part[u, 1, y_up].astype(bf16)
        near_send[u, 1, 0] = part[u, 0, y_down].astype(bf16)
        far_copy(u, 0, up).wait_recv()
        near_send[u, 0, 0] = (part[u, 0, y_up] + far_recv[u, 0].astype(f32)).astype(bf16)
        near_copy(u, 0, up).start()
        far_copy(u, 1, dn).wait_recv()
        near_send[u, 1, 1] = (part[u, 1, y_down] + far_recv[u, 1].astype(f32)).astype(bf16)
        near_copy(u, 1, dn).start()

    def home_copy(u, at):
        return remote(home_send.at[u], home.at[u, at], home_send_sem, home_recv_sem.at[u], across)

    def finish(u):
        m = u // CHUNKS
        near_copy(u, 0, up).wait_recv()
        near_copy(u, 1, dn).wait_recv()

        @pl.when(u == 0)
        def _():
            remote(gate_out.at[other], row_gate.at[0, other], gate_send_sem, gate_recv_sem, across).wait_recv()

        keep = jnp.where(m == 0, 1.0, 0.0)

        def summed(side):
            value = part[u, side, y] + near_recv[u, 0, side].astype(f32) + near_recv[u, 1, side].astype(f32)
            return (rows[u, side, y].astype(f32) * keep + value * row_gate[m, side][:, 0:1]).astype(bf16)

        home_send[u] = summed(other)
        home_copy(u, plane).start()
        home[u, plane] = summed(plane)

    def out_copy(u, out, j):
        return pltpu.make_async_copy(out_buf.at[u], out.at[:, columns(j)], out_sem)

    def deliver(u):
        home_copy(u, other).wait_recv()
        back = jnp.dot(unpick[u // CHUNKS], home[u].reshape(count, cw), preferred_element_type=f32)
        out_buf[u] = back.astype(bf16)

        @pl.when(u < CHUNKS)
        def _():
            out_copy(u, result, u).start()

        @pl.when(u >= CHUNKS)
        def _():
            out_copy(u, grad_in, u - CHUNKS).start()

    def at_step(i, behind, action):
        t = i - behind

        @pl.when((t >= 0) & (t < steps))
        def _():
            action(t)

    def gather_multiply(t):
        gathered(t)

        @pl.when(t < CHUNKS)
        def _():
            multiply_fwd(t)

        @pl.when(t >= CHUNKS)
        def _():
            multiply_bwd(t)

    def step(i, carry):
        at_step(i, 0, dispatch)
        at_step(i, 1, spread)
        at_step(i, 2, forward)
        at_step(i, 3, gather_multiply)
        at_step(i, START, produce)
        at_step(i, START + 1, add_far)
        at_step(i, START + 2, finish)
        at_step(i, START + 3, deliver)
        return carry

    lax.fori_loop(0, START + steps + 3, step, 0)

    for one in shares:
        one.wait_send()
    gate_copy.wait_send()
    pltpu.make_async_copy(arr, arr, pp_send).wait()
    narrow = rows.at[:, 0, 0]
    pltpu.make_async_copy(narrow, narrow, x_send).wait()
    for at in range(6):
        pltpu.make_async_copy(narrow, narrow, y_send.at[at]).wait()
    for way in range(2):
        pltpu.make_async_copy(narrow, narrow, far_send_sem.at[way]).wait()
        pltpu.make_async_copy(arr, arr, near_send_sem.at[way]).wait()
    pltpu.make_async_copy(narrow, narrow, home_send_sem).wait()
    pltpu.make_async_copy(arr, arr, out_sem).wait()


def local(
    section_out,
    routes_fwd,
    gates_fwd,
    cot_next,
    routes_bwd,
    gates_bwd,
    norm_gain,
    saved_gate,
    saved_up,
    w_gate,
    w_up,
    w_down,
):
    count, width = section_out.shape
    cap = count // EXPERTS
    unit = w_gate.shape[2]
    units = unit * CORES
    groups = EXPERTS * RING
    total = groups * cap
    cw = width // CHUNKS
    steps = 2 * CHUNKS
    held = (groups, CORES, cap, unit)
    f32, bf16 = jnp.float32, jnp.bfloat16
    vmem = pl.BlockSpec(memory_space=pltpu.VMEM)
    hbm = pl.BlockSpec(memory_space=pl.ANY)
    dma = pltpu.SemaphoreType.DMA
    return pl.pallas_call(
        kernel,
        out_shape=[jax.ShapeDtypeStruct((count, width), bf16)] * 2,
        in_specs=[hbm, hbm, vmem, vmem, vmem, vmem, vmem] + [hbm] * 5,
        out_specs=[hbm, hbm],
        scratch_shapes=[
            pltpu.VMEM((steps, count, cw), bf16),
            pltpu.VMEM((steps, EXPERTS, cap, cw), bf16),
            pltpu.VMEM((steps, EXPERTS, RING, cap, cw), bf16),
            pltpu.VMEM((width, 2 * units), bf16),
            pltpu.VMEM((units, width), bf16),
            pltpu.VMEM((groups, cap, units), bf16),
            pltpu.VMEM((groups, cap, units), bf16),
            pltpu.VMEM((2, count, count), bf16),
            pltpu.VMEM((2, count, count), bf16),
            pltpu.VMEM((2, count, 128), f32),
            pltpu.VMEM((2, EXPERTS, cap, 128), f32),
            pltpu.VMEM((EXPERTS, cap, 128), f32),
            pltpu.VMEM((total, 2 * units), f32),
            pltpu.VMEM((total, 128), f32),
            pltpu.VMEM((total, units), bf16),
            pltpu.VMEM((total, units), f32),
            pltpu.VMEM((total, 2 * units), bf16),
            pltpu.VMEM((steps, EXPERTS, RING, cap, cw), f32),
            pltpu.VMEM((steps, 2, cap, cw), bf16),
            pltpu.VMEM((steps, 2, cap, cw), bf16),
            pltpu.VMEM((steps, 2, EXPERTS, cap, cw), bf16),
            pltpu.VMEM((steps, 2, EXPERTS, cap, cw), bf16),
            pltpu.VMEM((steps, cap, cw), bf16),
            pltpu.VMEM((steps, EXPERTS, cap, cw), bf16),
            pltpu.VMEM((steps, count, cw), bf16),
            dma((5,)),
            dma((5,)),
            dma((5,)),
            dma,
            dma((steps,)),
            dma,
            dma((steps,)),
            dma((6,)),
            dma((steps, 6)),
            dma((2,)),
            dma((steps, 2)),
            dma((2,)),
            dma((steps, 2)),
            dma,
            dma((steps,)),
            dma,
            dma,
            dma,
        ],
        compiler_params=pltpu.CompilerParams(
            collective_id=0, has_side_effects=True, vmem_limit_bytes=56 * 1024 * 1024
        ),
        cost_estimate=pl.CostEstimate(
            flops=12 * total * width * units, bytes_accessed=16 * 1024 * 1024, transcendentals=2 * total * units
        ),
        name="relay_step",
    )(
        section_out,
        cot_next,
        routes_fwd.reshape(1, count),
        gates_fwd.reshape(1, count),
        routes_bwd.reshape(1, count),
        gates_bwd.reshape(1, count),
        norm_gain,
        saved_gate.reshape(held),
        saved_up.reshape(held),
        w_gate,
        w_up,
        w_down,
    )


def solution(mesh):
    in_specs = (
        P(("pp", "ep"), None),
        P(("pp", "ep"), None),
        P(("pp", "ep"), None),
        P(("pp", "ep"), None),
        P(("pp", "ep"), None),
        P(("pp", "ep"), None),
        P("pp", None),
        P("pp", None, "ep"),
        P("pp", None, "ep"),
        P("pp", None, "ep"),
        P("pp", None, "ep"),
        P("pp", "ep", None),
    )
    out_specs = (P(("pp", "ep"), None), P(("pp", "ep"), None))

    def whole(*args):
        first, second = jax.shard_map(
            local, mesh=mesh, in_specs=in_specs, out_specs=out_specs, check_vma=False
        )(*args)
        return first, second

    return whole
```

```python
import jax
import jax.numpy as jnp
from jax import lax
from jax.experimental import pallas as pl
from jax.experimental.pallas import tpu as pltpu
from jax.sharding import PartitionSpec as P

EXPERTS = 2
RING = 4
CORES = 2
LAYERS = 16
EPS = 1e-06
CHUNKS = 7
MESH = pl.DeviceIdType.MESH
TWIN_AT = 2
FWD_AT = 4
SPREAD = 1
FORWARD = 2
BWD_MULTIPLY_AT = 3
FWD_MULTIPLY_AT = 8
BWD_INNER_AT = 10
BWD_SUM_AT = (10, 12, 14, 18)
FWD_SUM_AT = (15, 18)
FWD, BWD, RELAY = 0, 1, 2


def kernel(
    section_out,
    cot_next,
    routes_fwd,
    gates_fwd,
    routes_bwd,
    gates_bwd,
    norm_gain,
    saved_gate,
    saved_up,
    w_gate,
    w_up,
    w_down,
    result,
    grad_in,
    leaving,
    arr,
    disp,
    rows_fwd,
    rows_bwd,
    gate_up,
    down,
    held_gate,
    held_up,
    pick,
    unpick,
    factor,
    act,
    squares,
    inner_send,
    inner,
    pair_grad,
    grad_send,
    grad_recv,
    inner_grad,
    both_grad,
    part_fwd,
    part_bwd,
    pair_send,
    pair_recv,
    far_send,
    far_recv,
    side_send,
    side_recv,
    own_send,
    own_recv,
    sums,
    out_buf,
    leaving_sem,
    load_sem,
    core_send,
    core_recv,
    pp_send,
    pp_recv,
    relay_send,
    x_send,
    x_recv,
    fwd_send,
    fwd_recv,
    bwd_send,
    bwd_recv,
    down_send,
    down_recv,
    down_core_send,
    down_core_recv,
    swap_send,
    swap_recv,
    pair_send_sem,
    pair_recv_sem,
    far_send_sem,
    far_recv_sem,
    side_send_sem,
    side_recv_sem,
    own_send_sem,
    own_recv_sem,
    out_sem,
    ready,
):
    count = section_out.shape[0]
    width = section_out.shape[1]
    cap = count // EXPERTS
    unit = w_gate.shape[2]
    units = unit * CORES
    cw = width // CHUNKS
    total = RING * count
    f32, bf16 = jnp.float32, jnp.bfloat16

    me_pp = lax.axis_index("pp")
    me = lax.axis_index("ep")
    n_pp = lax.axis_size("pp")
    layers = min(LAYERS, n_pp // 2)
    z = me_pp % layers
    z_base = me_pp - z
    wraps_up = (z + 1) // layers
    wraps_down = 1 - (z + layers - 1) // layers
    on_edge = (z == 0) | (z == layers - 1)
    plane = me // (RING * CORES)
    other = 1 - plane
    y = (me // CORES) % RING
    core = me % CORES
    half = y // 2
    side = y % 2
    y_a = y + 1 - 2 * side
    y_b = RING - 1 - y
    y_far = (y + 2) % RING

    def in_ring(at):
        return {"ep": plane * (RING * CORES) + at * CORES + core}

    chip_a = in_ring(y_a)
    chip_b = in_ring(y_b)
    across = {"ep": other * (RING * CORES) + y * CORES + core}
    across_a = {"ep": other * (RING * CORES) + y_a * CORES + core}
    across_b = {"ep": other * (RING * CORES) + y_b * CORES + core}
    twin = {"ep": plane * (RING * CORES) + y * CORES + (1 - core)}
    above = {"pp": z_base + (z + 1) % layers}
    below = {"pp": z_base + (z + layers - 1) % layers}
    mirror = {"pp": (me_pp + layers) % n_pp}

    barrier = pltpu.get_barrier_semaphore()

    def greet(**device):
        pl.semaphore_signal(barrier, inc=1, device_id=device, device_id_type=MESH)

    for at_plane, at_y in ((plane, y_a), (plane, y_b), (other, y), (other, y_a), (other, y_b)):
        greet(ep=at_plane * (RING * CORES) + at_y * CORES)
    pl.when(core == 1)(lambda: greet(ep=me - core))
    for section in (above, below, mirror):
        greet(pp=section["pp"], ep=me - core + 1)

    def tell(at):
        pl.semaphore_signal(ready.at[at], inc=1, device_id=twin, device_id_type=MESH)

    def columns(j):
        return pl.ds(pl.multiple_of(j * cw, cw), cw)

    def load_down(j):
        return pltpu.make_async_copy(w_down.at[0, :, columns(j)], down.at[j, core], load_sem.at[2])

    def load_rows(src, m, j):
        return pltpu.make_async_copy(src.at[:, columns(j)], leaving.at[m, j], leaving_sem.at[m])

    def start_loads(j, carry):
        load_rows(cot_next, BWD, j).start()
        load_rows(section_out, FWD, j).start()
        load_down(j).start()
        return carry

    lax.fori_loop(0, CHUNKS, start_loads, 0)
    loads = {}
    for at, (src, dst) in enumerate(
        [
            (w_gate.at[0], gate_up.at[core]),
            (w_up.at[0], gate_up.at[CORES + core]),
            (down.at[:, core], down.at[:, core]),
            (saved_gate.at[0, :, core], held_gate.at[core, :, 0]),
            (saved_gate.at[1, :, core], held_gate.at[core, :, 1]),
            (saved_up.at[0, :, core], held_up.at[core, :, 0]),
            (saved_up.at[1, :, core], held_up.at[core, :, 1]),
        ]
    ):
        loads[at] = pltpu.make_async_copy(src, dst, load_sem.at[at])
    for at in (0, 1, 3, 4, 5, 6):
        loads[at].start()
    @pl.when(core == 0)
    def _():
        pl.semaphore_wait(barrier, 5 * CORES + 1)
        tell(0)

    @pl.when(core == 1)
    def _():
        pl.semaphore_wait(ready.at[0], 1)

    loads[2].wait()

    def remote(src, dst, send, recv, to):
        return pltpu.make_async_remote_copy(
            src_ref=src, dst_ref=dst, send_sem=send, recv_sem=recv, device_id=to, device_id_type=MESH
        )

    def pp_copy(m, at, j, to):
        return remote(leaving.at[m, j], arr.at[at, j], pp_send, pp_recv.at[at, j], to)

    def down_copy(j):
        return remote(down.at[j, core], down.at[j, CORES + core], down_send, down_recv.at[j], chip_b)

    def start_down(j, carry):
        down_copy(j).start()
        return carry

    lax.fori_loop(0, CHUNKS, start_down, 0)

    def shared(src, dst, at):
        return remote(src, dst, core_send.at[at], core_recv.at[at], twin)

    shares = [
        shared(gate_up.at[core], gate_up.at[core], 0),
        shared(gate_up.at[CORES + core], gate_up.at[CORES + core], 1),
        shared(down.at[:, core], down.at[:, core], 2),
        shared(saved_gate.at[0, :, 1 - core], held_gate.at[core, :, 0], 3),
        shared(saved_gate.at[1, :, 1 - core], held_gate.at[core, :, 1], 4),
        shared(saved_up.at[0, :, 1 - core], held_up.at[core, :, 0], 5),
        shared(saved_up.at[1, :, 1 - core], held_up.at[core, :, 1], 6),
    ]
    for at in (2, 0, 1, 3, 4, 5, 6):
        if at < 2:
            loads[at].wait()
        shares[at].start()

    @pl.when(core == 1)
    def _():
        pl.semaphore_wait(barrier, 3 * CORES)
        tell(1)

    @pl.when(core == 0)
    def _():
        pl.semaphore_wait(ready.at[1], 1)

    for m in (BWD, FWD):
        pltpu.make_async_copy(leaving.at[m], leaving.at[m], leaving_sem.at[m]).wait()

    def start_first(j, carry):
        pp_copy(BWD, BWD + wraps_down, j, below).start()
        pp_copy(FWD, FWD + 2 * wraps_up, j, above).start()
        return carry

    lax.fori_loop(0, CHUNKS, start_first, 0)

    first = lax.broadcasted_iota(jnp.int32, (count, count), 0)
    second = lax.broadcasted_iota(jnp.int32, (count, count), 1)
    diagonal = first == second
    ones = jnp.ones((count, count), bf16)

    def places(routes, m):
        along = jnp.broadcast_to(routes[...].astype(f32), (count, count))
        down_rows = jnp.dot(jnp.where(diagonal, along, 0.0).astype(bf16), ones, preferred_element_type=f32)
        same = along == down_rows
        earlier = jnp.where(same & (first < second), 1.0, 0.0)
        place_along = along * cap + jnp.sum(earlier, axis=0, keepdims=True)
        chosen = place_along == first.astype(f32)
        pick[m] = jnp.where(chosen, 1.0, 0.0).astype(bf16)
        earlier = jnp.where(same & (second < first), 1.0, 0.0)
        place_down = down_rows * cap + jnp.sum(earlier, axis=1, keepdims=True)
        unpick[m] = jnp.where(place_down == second.astype(f32), 1.0, 0.0).astype(bf16)
        return chosen

    for m, routes, gates in ((BWD, routes_bwd, gates_bwd), (FWD, routes_fwd, gates_fwd)):
        chosen = places(routes, m)
        along = jnp.broadcast_to(gates[...], (count, count))
        slot_gate = jnp.sum(jnp.where(chosen, along, 0.0), axis=1, keepdims=True)
        factor[m] = jnp.broadcast_to(slot_gate, (count, 128))
    squares[...] = jnp.zeros_like(squares)
    act[...] = jnp.zeros_like(act)
    pair_grad[...] = jnp.zeros_like(pair_grad)

    def relay(j):
        @pl.when(on_edge)
        def _():
            pp_copy(FWD, RELAY, j, above).wait_recv()
            remote(arr.at[RELAY, j], arr.at[wraps_up, j], relay_send, pp_recv.at[wraps_up, j], mirror).start()

    def down_twin(j):
        down_copy(j).wait_recv()
        mine = down.at[j, CORES + core]
        remote(mine, mine, down_core_send, down_core_recv.at[j], twin).start()

    def cross(m, rows, at, j, sender):
        return remote(disp.at[m, j, other], rows.at[j, at, sender], x_send.at[m], x_recv.at[m, j], across)

    def bwd_copy(j, expert):
        mine = rows_bwd.at[j, side, expert]
        return remote(mine, mine, bwd_send.at[expert], bwd_recv.at[j, expert], chip_a)

    def bwd_arrival(j, expert):
        theirs = rows_bwd.at[j, 1 - side, expert]
        return remote(theirs, theirs, bwd_send.at[expert], bwd_recv.at[j, expert], chip_a)

    def dispatch_bwd(j):
        pp_copy(BWD, BWD, j, below).wait_recv()
        moved = jnp.dot(pick[BWD], arr[BWD, j], preferred_element_type=f32) * factor[BWD][:, 0:1]
        disp[BWD, j] = moved.astype(bf16).reshape(EXPERTS, cap, cw)
        cross(BWD, rows_bwd, side, j, plane).start()
        rows_bwd[j, side, plane] = disp[BWD, j, plane]
        bwd_copy(j, plane).start()

    def spread_bwd(j):
        cross(BWD, rows_bwd, side, j, other).wait_recv()
        bwd_copy(j, other).start()

    def fwd_copy(j, at, expert, to, sem):
        mine = rows_fwd.at[j, at, expert]
        return remote(mine, mine, fwd_send.at[sem], fwd_recv.at[j, sem], to)

    def pass_copy(j, at):
        block = rows_fwd.at[j, at]
        return remote(block, block, fwd_send.at[4], fwd_recv.at[j, 4], chip_a)

    def dispatch_fwd(j):
        pp_copy(FWD, FWD, j, above).wait_recv()
        moved = jnp.dot(pick[FWD], arr[FWD, j], preferred_element_type=f32)
        disp[FWD, j] = moved.astype(bf16).reshape(EXPERTS, cap, cw)
        cross(FWD, rows_fwd, y, j, plane).start()
        rows_fwd[j, y, plane] = disp[FWD, j, plane]
        fwd_copy(j, y, plane, chip_b, 2 + plane).start()
        fwd_copy(j, y, plane, chip_a, plane).start()

    def spread_fwd(j):
        cross(FWD, rows_fwd, y, j, other).wait_recv()
        fwd_copy(j, y, other, chip_b, 2 + other).start()
        fwd_copy(j, y, other, chip_a, other).start()

    def forward_fwd(j):
        for expert in range(EXPERTS):
            fwd_copy(j, y_b, expert, chip_b, 2 + expert).wait_recv()
        pass_copy(j, y_b).start()

    def wait_loads(which):
        for at in which:
            if at > 2:
                loads[at].wait()
            shares[at].wait_recv()

    def both_weights(j):
        return jnp.concatenate([gate_up[at, columns(j), :] for at in range(2 * CORES)], axis=1)

    def all_units(held):
        return jnp.concatenate([held[at].reshape(total, unit) for at in range(CORES)], axis=1).astype(f32)

    def grad_swap():
        return remote(grad_send, grad_recv, swap_send.at[BWD], swap_recv.at[BWD], chip_b)

    def inner_swap():
        return remote(
            inner_send, inner.at[:, :, units : 2 * units], swap_send.at[FWD], swap_recv.at[FWD], chip_b
        )

    def multiply_bwd(j):
        @pl.when(j == 0)
        def _():
            wait_loads((2,))

        for expert in range(EXPERTS):
            bwd_arrival(j, expert).wait_recv()
        theirs = down.at[j, CORES + 1 - core]
        remote(theirs, theirs, down_core_send, down_core_recv.at[j], twin).wait_recv()
        pair_grad[...] += lax.dot_general(
            rows_bwd[j].reshape(2 * count, cw),
            down[j].reshape(2 * units, cw),
            (((1,), (1,)), ((), ())),
            preferred_element_type=f32,
        )

        @pl.when(j == CHUNKS - 1)
        def _():
            grad_send[...] = pair_grad[:, units : 2 * units].astype(bf16).reshape(2, count, units)
            grad_swap().start()
            inner_grad[pl.ds(2 * half, 2)] = pair_grad[:, 0:units].reshape(2, count, units)

    def finish_inner_grad():
        wait_loads((3, 4, 5, 6))
        grad_swap().wait_recv()
        inner_grad[pl.ds(2 * (1 - half), 2)] = grad_recv[...].astype(f32)
        grad = inner_grad[...].reshape(total, units)
        gate_act = all_units(held_gate)
        up_act = all_units(held_up)
        sigma = jax.nn.sigmoid(gate_act)
        both_grad[:, 0:units] = (grad * up_act * sigma * (1.0 + gate_act * (1.0 - sigma))).astype(bf16)
        both_grad[:, units : 2 * units] = (grad * gate_act * sigma).astype(bf16)

    def multiply_fwd(j):
        @pl.when(j == 0)
        def _():
            wait_loads((0, 1))

        for expert in range(EXPERTS):
            fwd_copy(j, y_a, expert, chip_a, expert).wait_recv()
        pass_copy(j, y_far).wait_recv()
        floats = rows_fwd[j].reshape(total, cw).astype(f32)
        squared = floats * floats
        summed = squared[:, 0:128]
        for k in range(1, cw // 128):
            summed = summed + squared[:, k * 128 : (k + 1) * 128]
        squares[...] += summed
        left = (floats * norm_gain[:, columns(j)]).astype(bf16)
        act[...] += jnp.dot(left, both_weights(j), preferred_element_type=f32)

        @pl.when(j == CHUNKS - 1)
        def _():
            mean = jnp.sum(squares[...], axis=1, keepdims=True) * (1.0 / width)
            scale = lax.rsqrt(mean + EPS)
            gate_act = act[:, 0:units] * scale
            up_act = act[:, units : 2 * units] * scale
            value = (gate_act * jax.nn.sigmoid(gate_act) * up_act).astype(bf16).reshape(2, 2, count, units)
            for at in range(2):
                @pl.when(half == at)
                def _():
                    inner[:, :, 0:units] = value[at]
                    inner_send[...] = value[1 - at]
            inner_swap().start()

    def far_copy(j):
        return remote(far_send.at[j], far_recv.at[j], far_send_sem, far_recv_sem.at[j], chip_b)

    def side_copy(j, way, expert, sender, to):
        return remote(
            side_send.at[way, j, expert],
            side_recv.at[way, j, sender],
            side_send_sem.at[way],
            side_recv_sem.at[way, j, sender],
            to,
        )

    def own_copy(m, j):
        return remote(own_send.at[m, j], own_recv.at[m, j], own_send_sem.at[m], own_recv_sem.at[m, j], across)

    def produce_bwd(j):
        value = lax.dot_general(
            both_grad[...], both_weights(j), (((1,), (1,)), ((), ())), preferred_element_type=f32
        )
        part_bwd[j] = value.reshape(RING, EXPERTS, cap, cw)
        far_send[j] = part_bwd[j, y_far].astype(bf16)
        far_copy(j).start()
        own_send[BWD, j] = part_bwd[j, y, other].astype(bf16)
        own_copy(BWD, j).start()
        side_send[1, j] = part_bwd[j, y_b].astype(bf16)

    def send_side(j):
        side_copy(j, 1, plane, plane, chip_b).start()
        side_copy(j, 1, other, plane, across_b).start()

    def add_bwd(j):
        far_copy(j).wait_recv()
        side_send[0, j] = (part_bwd[j, y_a] + far_recv[j].astype(f32)).astype(bf16)
        side_copy(j, 0, plane, plane, chip_a).start()
        side_copy(j, 0, other, plane, across_a).start()

    def pair_copy(j, expert, sender, to):
        return remote(pair_send.at[j, expert], pair_recv.at[j, sender], pair_send_sem, pair_recv_sem.at[j, sender], to)

    def produce_fwd(j):
        @pl.when(j == 0)
        def _():
            inner_swap().wait_recv()

        value = jnp.dot(
            inner[...].reshape(2 * count, 2 * units), down[j].reshape(2 * units, cw), preferred_element_type=f32
        )
        part_fwd[j] = value.reshape(2, EXPERTS, cap, cw)
        pair_send[j] = part_fwd[j, 1 - side].astype(bf16)
        pair_copy(j, plane, plane, chip_a).start()
        pair_copy(j, other, plane, across_a).start()
        own_send[FWD, j] = part_fwd[j, side, other].astype(bf16)
        own_copy(FWD, j).start()

    def out_copy(m, out, j):
        return pltpu.make_async_copy(out_buf.at[m, j], out.at[:, columns(j)], out_sem.at[m])

    def deliver(m, out, j, slots):
        back = jnp.dot(unpick[m], slots.reshape(count, cw), preferred_element_type=f32)
        out_buf[m, j] = back.astype(bf16)
        out_copy(m, out, j).start()

    def finish_bwd(j):
        own_copy(BWD, j).wait_recv()
        for way, here, there in ((0, chip_a, across_a), (1, chip_b, across_b)):
            side_copy(j, way, plane, plane, here).wait_recv()
            side_copy(j, way, other, other, there).wait_recv()
        sums[plane] = part_bwd[j, y, plane]
        sums[other] = own_recv[BWD, j].astype(f32)
        value = sums[...] + side_recv[0, j].astype(f32) + side_recv[1, j].astype(f32)
        deliver(BWD, grad_in, j, value.astype(bf16))

    def finish_fwd(j):
        own_copy(FWD, j).wait_recv()
        pair_copy(j, plane, plane, chip_a).wait_recv()
        pair_copy(j, other, other, across_a).wait_recv()
        sums[plane] = part_fwd[j, side, plane]
        sums[other] = own_recv[FWD, j].astype(f32)
        value = (sums[...] + pair_recv[j].astype(f32)).reshape(count, cw) * factor[FWD][:, 0:1]
        deliver(FWD, result, j, (disp[FWD, j].astype(f32).reshape(count, cw) + value).astype(bf16))

    def at_step(i, start, action):
        j = i - start

        @pl.when((j >= 0) & (j < CHUNKS))
        def _():
            action(j)

    relay(0)

    def step(i, carry):
        at_step(i + 1, 1, lambda j: pl.when(j + 1 < CHUNKS)(lambda: relay(j + 1)))
        at_step(i, TWIN_AT, down_twin)
        at_step(i, 0, dispatch_bwd)
        at_step(i, FWD_AT, dispatch_fwd)
        at_step(i, SPREAD, spread_bwd)
        at_step(i, FWD_AT + SPREAD, spread_fwd)
        at_step(i, FWD_AT + FORWARD, forward_fwd)
        at_step(i, BWD_MULTIPLY_AT, multiply_bwd)
        at_step(i, FWD_MULTIPLY_AT, multiply_fwd)
        pl.when(i == BWD_INNER_AT)(finish_inner_grad)
        at_step(i, BWD_SUM_AT[0], produce_bwd)
        at_step(i, BWD_SUM_AT[1], add_bwd)
        at_step(i, BWD_SUM_AT[2], send_side)
        at_step(i, FWD_SUM_AT[0], produce_fwd)
        at_step(i, FWD_SUM_AT[1], finish_fwd)
        at_step(i, BWD_SUM_AT[3], finish_bwd)
        return carry

    lax.fori_loop(0, max(BWD_SUM_AT[3], FWD_SUM_AT[1]) + CHUNKS, step, 0)

    for one in shares:
        one.wait_send()
    grad_swap().wait_send()
    inner_swap().wait_send()

    def sent(ref, sem):
        pltpu.make_async_copy(ref, ref, sem).wait()

    sent(arr.at[0:2], pp_send)
    pl.when(on_edge)(lambda: sent(arr.at[0], relay_send))
    sent(down.at[:, 0], down_send)
    sent(down.at[:, 0], down_core_send)
    narrow = disp.at[0, :, 0]
    for m in range(2):
        sent(narrow, x_send.at[m])
        sent(narrow, bwd_send.at[m])
        sent(narrow, own_send_sem.at[m])
        sent(out_buf.at[m], out_sem.at[m])
        sent(side_send.at[m], side_send_sem.at[m])
    for at in range(4):
        sent(narrow, fwd_send.at[at])
    sent(pair_send, fwd_send.at[4])
    sent(pair_send, pair_send_sem)
    sent(far_send, far_send_sem)


def local(
    section_out,
    routes_fwd,
    gates_fwd,
    cot_next,
    routes_bwd,
    gates_bwd,
    norm_gain,
    saved_gate,
    saved_up,
    w_gate,
    w_up,
    w_down,
):
    count, width = section_out.shape
    cap = count // EXPERTS
    unit = w_gate.shape[2]
    units = unit * CORES
    total = RING * count
    cw = width // CHUNKS
    held = (EXPERTS, RING, CORES, cap, unit)
    f32, bf16 = jnp.float32, jnp.bfloat16
    vmem = pl.BlockSpec(memory_space=pltpu.VMEM)
    hbm = pl.BlockSpec(memory_space=pl.ANY)
    dma = pltpu.SemaphoreType.DMA
    block = (EXPERTS, cap, cw)
    return pl.pallas_call(
        kernel,
        out_shape=[jax.ShapeDtypeStruct((count, width), bf16)] * 2,
        in_specs=[hbm, hbm, vmem, vmem, vmem, vmem, vmem] + [hbm] * 5,
        out_specs=[hbm, hbm],
        scratch_shapes=[
            pltpu.VMEM((2, CHUNKS, count, cw), bf16),
            pltpu.VMEM((3, CHUNKS, count, cw), bf16),
            pltpu.VMEM((2, CHUNKS) + block, bf16),
            pltpu.VMEM((CHUNKS, RING) + block, bf16),
            pltpu.VMEM((CHUNKS, 2) + block, bf16),
            pltpu.VMEM((2 * CORES, width, unit), bf16),
            pltpu.VMEM((CHUNKS, 2 * CORES, unit, cw), bf16),
            pltpu.VMEM((CORES, RING, EXPERTS, cap, unit), bf16),
            pltpu.VMEM((CORES, RING, EXPERTS, cap, unit), bf16),
            pltpu.VMEM((2, count, count), bf16),
            pltpu.VMEM((2, count, count), bf16),
            pltpu.VMEM((2, count, 128), f32),
            pltpu.VMEM((total, 2 * units), f32),
            pltpu.VMEM((total, 128), f32),
            pltpu.VMEM((2, count, units), bf16),
            pltpu.VMEM((2, count, 2 * units), bf16),
            pltpu.VMEM((2 * count, 2 * units), f32),
            pltpu.VMEM((2, count, units), bf16),
            pltpu.VMEM((2, count, units), bf16),
            pltpu.VMEM((RING, count, units), f32),
            pltpu.VMEM((total, 2 * units), bf16),
            pltpu.VMEM((CHUNKS, 2) + block, f32),
            pltpu.VMEM((CHUNKS, RING) + block, f32),
            pltpu.VMEM((CHUNKS,) + block, bf16),
            pltpu.VMEM((CHUNKS,) + block, bf16),
            pltpu.VMEM((CHUNKS,) + block, bf16),
            pltpu.VMEM((CHUNKS,) + block, bf16),
            pltpu.VMEM((2, CHUNKS) + block, bf16),
            pltpu.VMEM((2, CHUNKS) + block, bf16),
            pltpu.VMEM((2, CHUNKS, cap, cw), bf16),
            pltpu.VMEM((2, CHUNKS, cap, cw), bf16),
            pltpu.VMEM(block, f32),
            pltpu.VMEM((2, CHUNKS, count, cw), bf16),
            dma((2,)),
            dma((7,)),
            dma((7,)),
            dma((7,)),
            dma,
            dma((3, CHUNKS)),
            dma,
            dma((2,)),
            dma((2, CHUNKS)),
            dma((5,)),
            dma((CHUNKS, 5)),
            dma((2,)),
            dma((CHUNKS, 2)),
            dma,
            dma((CHUNKS,)),
            dma,
            dma((CHUNKS,)),
            dma((2,)),
            dma((2,)),
            dma,
            dma((CHUNKS, EXPERTS)),
            dma,
            dma((CHUNKS,)),
            dma((2,)),
            dma((2, CHUNKS, EXPERTS)),
            dma((2,)),
            dma((2, CHUNKS)),
            dma((2,)),
            pltpu.SemaphoreType.REGULAR((2,)),
        ],
        compiler_params=pltpu.CompilerParams(
            collective_id=0, has_side_effects=True, vmem_limit_bytes=58 * 1024 * 1024
        ),
        cost_estimate=pl.CostEstimate(
            flops=12 * total * width * units, bytes_accessed=16 * 1024 * 1024, transcendentals=2 * total * units
        ),
        name="relay_step",
    )(
        section_out,
        cot_next,
        routes_fwd.reshape(1, count),
        gates_fwd.reshape(1, count),
        routes_bwd.reshape(1, count),
        gates_bwd.reshape(1, count),
        norm_gain,
        saved_gate.reshape(held),
        saved_up.reshape(held),
        w_gate,
        w_up,
        w_down,
    )


def solution(mesh):
    in_specs = (
        P(("pp", "ep"), None),
        P(("pp", "ep"), None),
        P(("pp", "ep"), None),
        P(("pp", "ep"), None),
        P(("pp", "ep"), None),
        P(("pp", "ep"), None),
        P("pp", None),
        P("pp", None, "ep"),
        P("pp", None, "ep"),
        P("pp", None, "ep"),
        P("pp", None, "ep"),
        P("pp", "ep", None),
    )
    out_specs = (P(("pp", "ep"), None), P(("pp", "ep"), None))

    def whole(*args):
        first, second = jax.shard_map(
            local, mesh=mesh, in_specs=in_specs, out_specs=out_specs, check_vma=False
        )(*args)
        return first, second

    return whole
```

```python
import jax
import jax.numpy as jnp
from jax import lax
from jax.experimental import pallas as pl
from jax.experimental.pallas import tpu as pltpu
from jax.sharding import PartitionSpec as P

EXPERTS = 2
RING = 4
CORES = 2
LAYERS = 16
EPS = 1e-06
CHUNKS = 4
MESH = pl.DeviceIdType.MESH
RELAY_AT = 1
TWIN_AT = 1
FWD_AT = 2
SPREAD = 1
FORWARD = 2
BWD_MULTIPLY_AT = 2
FWD_MULTIPLY_AT = 5
BWD_INNER_AT = 6
BWD_SUM_AT = (6, 8, 9, 11)
FWD_SUM_AT = (9, 11)
FWD, BWD, RELAY = 0, 1, 2


def kernel(
    section_out,
    cot_next,
    routes_fwd,
    gates_fwd,
    routes_bwd,
    gates_bwd,
    norm_gain,
    saved_gate,
    saved_up,
    w_gate,
    w_up,
    w_down,
    result,
    grad_in,
    leaving,
    arr,
    disp,
    rows_fwd,
    rows_bwd,
    gate_up,
    down,
    held_gate,
    held_up,
    pick,
    unpick,
    factor,
    act,
    squares,
    inner_send,
    inner,
    pair_grad,
    grad_send,
    grad_recv,
    inner_grad,
    both_grad,
    part_fwd,
    part_bwd,
    pair_send,
    pair_recv,
    far_send,
    far_recv,
    side_send,
    side_recv,
    own_send,
    own_recv,
    sums,
    out_buf,
    leaving_sem,
    load_sem,
    core_send,
    core_recv,
    pp_send,
    pp_recv,
    relay_send,
    x_send,
    x_recv,
    fwd_send,
    fwd_recv,
    bwd_send,
    bwd_recv,
    down_send,
    down_recv,
    down_core_send,
    down_core_recv,
    swap_send,
    swap_recv,
    pair_send_sem,
    pair_recv_sem,
    far_send_sem,
    far_recv_sem,
    side_send_sem,
    side_recv_sem,
    own_send_sem,
    own_recv_sem,
    out_sem,
    ready,
):
    count = section_out.shape[0]
    width = section_out.shape[1]
    cap = count // EXPERTS
    unit = w_gate.shape[2]
    units = unit * CORES
    cw = width // CHUNKS
    total = RING * count
    f32, bf16 = jnp.float32, jnp.bfloat16

    me_pp = lax.axis_index("pp")
    me = lax.axis_index("ep")
    n_pp = lax.axis_size("pp")
    layers = min(LAYERS, n_pp // 2)
    z = me_pp % layers
    z_base = me_pp - z
    wraps_up = (z + 1) // layers
    wraps_down = 1 - (z + layers - 1) // layers
    on_edge = (z == 0) | (z == layers - 1)
    split_way = z == 0
    plane = me // (RING * CORES)
    other = 1 - plane
    y = (me // CORES) % RING
    core = me % CORES
    half = y // 2
    side = y % 2
    y_a = y + 1 - 2 * side
    y_b = RING - 1 - y
    y_far = (y + 2) % RING

    def in_ring(at):
        return {"ep": plane * (RING * CORES) + at * CORES + core}

    chip_a = in_ring(y_a)
    chip_b = in_ring(y_b)
    across = {"ep": other * (RING * CORES) + y * CORES + core}
    across_a = {"ep": other * (RING * CORES) + y_a * CORES + core}
    across_b = {"ep": other * (RING * CORES) + y_b * CORES + core}
    twin = {"ep": plane * (RING * CORES) + y * CORES + (1 - core)}
    above = {"pp": z_base + (z + 1) % layers}
    below = {"pp": z_base + (z + layers - 1) % layers}
    mirror = {"pp": (me_pp + layers) % n_pp}

    barrier = pltpu.get_barrier_semaphore()

    def greet(**device):
        pl.semaphore_signal(barrier, inc=1, device_id=device, device_id_type=MESH)

    for at_plane, at_y in ((plane, y_a), (plane, y_b), (other, y), (other, y_a), (other, y_b)):
        greet(ep=at_plane * (RING * CORES) + at_y * CORES)
    pl.when(core == 1)(lambda: greet(ep=me - core))
    for section in (above, below, mirror):
        greet(pp=section["pp"], ep=me - core + 1)

    def tell(at):
        pl.semaphore_signal(ready.at[at], inc=1, device_id=twin, device_id_type=MESH)

    def columns(j):
        return pl.ds(pl.multiple_of(j * cw, cw), cw)

    def load_down(j):
        return pltpu.make_async_copy(w_down.at[0, :, columns(j)], down.at[j, core], load_sem.at[2])

    def load_rows(src, m, j):
        return pltpu.make_async_copy(src.at[:, columns(j)], leaving.at[m, j], leaving_sem.at[m])

    def start_loads(j, carry):
        load_rows(cot_next, BWD, j).start()
        load_rows(section_out, FWD, j).start()
        load_down(j).start()
        return carry

    lax.fori_loop(0, CHUNKS, start_loads, 0)
    loads = {}
    for at, (src, dst) in enumerate(
        [
            (w_gate.at[0], gate_up.at[core]),
            (w_up.at[0], gate_up.at[CORES + core]),
            (down.at[:, core], down.at[:, core]),
            (saved_gate.at[0, :, core], held_gate.at[core, :, 0]),
            (saved_gate.at[1, :, core], held_gate.at[core, :, 1]),
            (saved_up.at[0, :, core], held_up.at[core, :, 0]),
            (saved_up.at[1, :, core], held_up.at[core, :, 1]),
        ]
    ):
        loads[at] = pltpu.make_async_copy(src, dst, load_sem.at[at])
    for at in (0, 1, 3, 4, 5, 6):
        loads[at].start()
    @pl.when(core == 0)
    def _():
        pl.semaphore_wait(barrier, 5 * CORES + 1)
        tell(0)

    @pl.when(core == 1)
    def _():
        pl.semaphore_wait(ready.at[0], 1)

    loads[2].wait()

    def remote(src, dst, send, recv, to):
        return pltpu.make_async_remote_copy(
            src_ref=src, dst_ref=dst, send_sem=send, recv_sem=recv, device_id=to, device_id_type=MESH
        )

    def pp_copy(m, at, j, to):
        return remote(leaving.at[m, j], arr.at[at, j], pp_send, pp_recv.at[at, j], to)

    def down_copy(j):
        return remote(down.at[j, core], down.at[j, CORES + core], down_send, down_recv.at[j], chip_b)

    def start_down(j, carry):
        down_copy(j).start()
        return carry

    lax.fori_loop(0, CHUNKS, start_down, 0)

    def shared(src, dst, at):
        return remote(src, dst, core_send.at[at], core_recv.at[at], twin)

    shares = [
        shared(gate_up.at[core], gate_up.at[core], 0),
        shared(gate_up.at[CORES + core], gate_up.at[CORES + core], 1),
        shared(down.at[:, core], down.at[:, core], 2),
        shared(saved_gate.at[0, :, 1 - core], held_gate.at[core, :, 0], 3),
        shared(saved_gate.at[1, :, 1 - core], held_gate.at[core, :, 1], 4),
        shared(saved_up.at[0, :, 1 - core], held_up.at[core, :, 0], 5),
        shared(saved_up.at[1, :, 1 - core], held_up.at[core, :, 1], 6),
    ]
    for at in (2, 0, 1, 3, 4, 5, 6):
        if at < 2:
            loads[at].wait()
        shares[at].start()

    @pl.when(core == 1)
    def _():
        pl.semaphore_wait(barrier, 3 * CORES)
        tell(1)

    @pl.when(core == 0)
    def _():
        pl.semaphore_wait(ready.at[1], 1)

    for m in (BWD, FWD):
        pltpu.make_async_copy(leaving.at[m], leaving.at[m], leaving_sem.at[m]).wait()

    def start_first(j, carry):
        pp_copy(BWD, BWD + wraps_down, j, below).start()
        pp_copy(FWD, FWD + 2 * wraps_up, j, above).start()
        return carry

    lax.fori_loop(0, CHUNKS, start_first, 0)

    first = lax.broadcasted_iota(jnp.int32, (count, count), 0)
    second = lax.broadcasted_iota(jnp.int32, (count, count), 1)
    diagonal = first == second
    ones = jnp.ones((count, count), bf16)

    def places(routes, m):
        along = jnp.broadcast_to(routes[...].astype(f32), (count, count))
        down_rows = jnp.dot(jnp.where(diagonal, along, 0.0).astype(bf16), ones, preferred_element_type=f32)
        same = along == down_rows
        earlier = jnp.where(same & (first < second), 1.0, 0.0)
        place_along = along * cap + jnp.sum(earlier, axis=0, keepdims=True)
        chosen = place_along == first.astype(f32)
        pick[m] = jnp.where(chosen, 1.0, 0.0).astype(bf16)
        earlier = jnp.where(same & (second < first), 1.0, 0.0)
        place_down = down_rows * cap + jnp.sum(earlier, axis=1, keepdims=True)
        unpick[m] = jnp.where(place_down == second.astype(f32), 1.0, 0.0).astype(bf16)
        return chosen

    for m, routes, gates in ((BWD, routes_bwd, gates_bwd), (FWD, routes_fwd, gates_fwd)):
        chosen = places(routes, m)
        along = jnp.broadcast_to(gates[...], (count, count))
        slot_gate = jnp.sum(jnp.where(chosen, along, 0.0), axis=1, keepdims=True)
        factor[m] = jnp.broadcast_to(slot_gate, (count, 128))
    squares[...] = jnp.zeros_like(squares)
    act[...] = jnp.zeros_like(act)
    pair_grad[...] = jnp.zeros_like(pair_grad)

    def relay(j, m):
        pp_copy(FWD, RELAY, j, above).wait_recv()
        remote(arr.at[RELAY, j], arr.at[m, j], relay_send, pp_recv.at[m, j], mirror).start()

    def relay_fwd(j):
        pl.when(z == 0)(lambda: relay(j, FWD))

    def relay_bwd(j):
        pl.when(z == layers - 1)(lambda: relay(j, BWD))

    def down_twin(j):
        down_copy(j).wait_recv()
        mine = down.at[j, CORES + core]
        remote(mine, mine, down_core_send, down_core_recv.at[j], twin).start()

    def cross(m, rows, at, j, sender):
        return remote(disp.at[m, j, other], rows.at[j, at, sender], x_send.at[m], x_recv.at[m, j], across)

    def bwd_copy(j, expert):
        mine = rows_bwd.at[j, side, expert]
        return remote(mine, mine, bwd_send.at[expert], bwd_recv.at[j, expert], chip_a)

    def bwd_arrival(j, expert):
        theirs = rows_bwd.at[j, 1 - side, expert]
        return remote(theirs, theirs, bwd_send.at[expert], bwd_recv.at[j, expert], chip_a)

    def dispatch_bwd(j):
        pp_copy(BWD, BWD, j, below).wait_recv()
        moved = jnp.dot(pick[BWD], arr[BWD, j], preferred_element_type=f32) * factor[BWD][:, 0:1]
        disp[BWD, j] = moved.astype(bf16).reshape(EXPERTS, cap, cw)
        cross(BWD, rows_bwd, side, j, plane).start()
        rows_bwd[j, side, plane] = disp[BWD, j, plane]
        bwd_copy(j, plane).start()

    def spread_bwd(j):
        cross(BWD, rows_bwd, side, j, other).wait_recv()
        bwd_copy(j, other).start()

    def fwd_copy(j, at, expert, to, sem):
        mine = rows_fwd.at[j, at, expert]
        return remote(mine, mine, fwd_send.at[sem], fwd_recv.at[j, sem], to)

    def pass_copy(j, at, expert, to):
        block = rows_fwd.at[j, at, expert]
        return remote(block, block, fwd_send.at[4], fwd_recv.at[j, 4 + expert], to)

    def dispatch_fwd(j):
        pp_copy(FWD, FWD, j, above).wait_recv()
        moved = jnp.dot(pick[FWD], arr[FWD, j], preferred_element_type=f32)
        disp[FWD, j] = moved.astype(bf16).reshape(EXPERTS, cap, cw)
        cross(FWD, rows_fwd, y, j, plane).start()
        rows_fwd[j, y, plane] = disp[FWD, j, plane]
        fwd_copy(j, y, plane, chip_b, 2 + plane).start()
        fwd_copy(j, y, plane, chip_a, plane).start()

    def spread_fwd(j):
        cross(FWD, rows_fwd, y, j, other).wait_recv()
        fwd_copy(j, y, other, chip_b, 2 + other).start()
        fwd_copy(j, y, other, chip_a, other).start()

    def forward_fwd(j):
        fwd_copy(j, y_b, 0, chip_b, 2).wait_recv()
        pass_copy(j, y_b, 0, chip_a).start()

        @pl.when(split_way)
        def _():
            fwd_copy(j, y_a, 1, chip_a, 1).wait_recv()
            pass_copy(j, y_a, 1, chip_b).start()

        @pl.when(jnp.logical_not(split_way))
        def _():
            fwd_copy(j, y_b, 1, chip_b, 3).wait_recv()
            pass_copy(j, y_b, 1, chip_a).start()

    def wait_loads(which):
        for at in which:
            if at > 2:
                loads[at].wait()
            shares[at].wait_recv()

    def both_weights(j):
        return jnp.concatenate([gate_up[at, columns(j), :] for at in range(2 * CORES)], axis=1)

    def all_units(held):
        return jnp.concatenate([held[at].reshape(total, unit) for at in range(CORES)], axis=1).astype(f32)

    def grad_swap():
        return remote(grad_send, grad_recv, swap_send.at[BWD], swap_recv.at[BWD], chip_b)

    def inner_swap():
        return remote(
            inner_send, inner.at[:, :, units : 2 * units], swap_send.at[FWD], swap_recv.at[FWD], chip_b
        )

    def multiply_bwd(j):
        @pl.when(j == 0)
        def _():
            wait_loads((2,))

        for expert in range(EXPERTS):
            bwd_arrival(j, expert).wait_recv()
        theirs = down.at[j, CORES + 1 - core]
        remote(theirs, theirs, down_core_send, down_core_recv.at[j], twin).wait_recv()
        pair_grad[...] += lax.dot_general(
            rows_bwd[j].reshape(2 * count, cw),
            down[j].reshape(2 * units, cw),
            (((1,), (1,)), ((), ())),
            preferred_element_type=f32,
        )

        @pl.when(j == CHUNKS - 1)
        def _():
            grad_send[...] = pair_grad[:, units : 2 * units].astype(bf16).reshape(2, count, units)
            grad_swap().start()
            inner_grad[pl.ds(2 * half, 2)] = pair_grad[:, 0:units].reshape(2, count, units)

    def finish_inner_grad():
        wait_loads((3, 4, 5, 6))
        grad_swap().wait_recv()
        inner_grad[pl.ds(2 * (1 - half), 2)] = grad_recv[...].astype(f32)
        grad = inner_grad[...].reshape(total, units)
        gate_act = all_units(held_gate)
        up_act = all_units(held_up)
        sigma = jax.nn.sigmoid(gate_act)
        both_grad[:, 0:units] = (grad * up_act * sigma * (1.0 + gate_act * (1.0 - sigma))).astype(bf16)
        both_grad[:, units : 2 * units] = (grad * gate_act * sigma).astype(bf16)

    def multiply_fwd(j):
        @pl.when(j == 0)
        def _():
            wait_loads((0, 1))

        fwd_copy(j, y_a, 0, chip_a, 0).wait_recv()

        @pl.when(split_way)
        def _():
            fwd_copy(j, y_b, 1, chip_b, 3).wait_recv()

        @pl.when(jnp.logical_not(split_way))
        def _():
            fwd_copy(j, y_a, 1, chip_a, 1).wait_recv()

        for expert in range(EXPERTS):
            pass_copy(j, y_far, expert, chip_a).wait_recv()
        floats = rows_fwd[j].reshape(total, cw).astype(f32)
        squared = floats * floats
        summed = squared[:, 0:128]
        for k in range(1, cw // 128):
            summed = summed + squared[:, k * 128 : (k + 1) * 128]
        squares[...] += summed
        left = (floats * norm_gain[:, columns(j)]).astype(bf16)
        act[...] += jnp.dot(left, both_weights(j), preferred_element_type=f32)

        @pl.when(j == CHUNKS - 1)
        def _():
            mean = jnp.sum(squares[...], axis=1, keepdims=True) * (1.0 / width)
            scale = lax.rsqrt(mean + EPS)
            gate_act = act[:, 0:units] * scale
            up_act = act[:, units : 2 * units] * scale
            value = (gate_act * jax.nn.sigmoid(gate_act) * up_act).astype(bf16).reshape(2, 2, count, units)
            for at in range(2):
                @pl.when(half == at)
                def _():
                    inner[:, :, 0:units] = value[at]
                    inner_send[...] = value[1 - at]
            inner_swap().start()

    def far_copy(j):
        return remote(far_send.at[j], far_recv.at[j], far_send_sem, far_recv_sem.at[j], chip_b)

    def side_copy(j, way, expert, sender, to):
        return remote(
            side_send.at[way, j, expert],
            side_recv.at[way, j, sender],
            side_send_sem.at[way],
            side_recv_sem.at[way, j, sender],
            to,
        )

    def own_copy(m, j):
        return remote(own_send.at[m, j], own_recv.at[m, j], own_send_sem.at[m], own_recv_sem.at[m, j], across)

    def produce_bwd(j):
        value = lax.dot_general(
            both_grad[...], both_weights(j), (((1,), (1,)), ((), ())), preferred_element_type=f32
        )
        part_bwd[j] = value.reshape(RING, EXPERTS, cap, cw)
        far_send[j] = part_bwd[j, y_far].astype(bf16)
        far_copy(j).start()
        own_send[BWD, j] = part_bwd[j, y, other].astype(bf16)
        own_copy(BWD, j).start()
        side_send[1, j] = part_bwd[j, y_b].astype(bf16)

    def send_side(j):
        side_copy(j, 1, plane, plane, chip_b).start()
        side_copy(j, 1, other, plane, across_b).start()

    def add_bwd(j):
        far_copy(j).wait_recv()
        side_send[0, j] = (part_bwd[j, y_a] + far_recv[j].astype(f32)).astype(bf16)
        side_copy(j, 0, plane, plane, chip_a).start()
        side_copy(j, 0, other, plane, across_a).start()

    def pair_copy(j, expert, sender, to):
        return remote(pair_send.at[j, expert], pair_recv.at[j, sender], pair_send_sem, pair_recv_sem.at[j, sender], to)

    def produce_fwd(j):
        @pl.when(j == 0)
        def _():
            inner_swap().wait_recv()

        value = jnp.dot(
            inner[...].reshape(2 * count, 2 * units), down[j].reshape(2 * units, cw), preferred_element_type=f32
        )
        part_fwd[j] = value.reshape(2, EXPERTS, cap, cw)
        pair_send[j] = part_fwd[j, 1 - side].astype(bf16)
        pair_copy(j, plane, plane, chip_a).start()
        pair_copy(j, other, plane, across_a).start()
        own_send[FWD, j] = part_fwd[j, side, other].astype(bf16)
        own_copy(FWD, j).start()

    def out_copy(m, out, j):
        return pltpu.make_async_copy(out_buf.at[m, j], out.at[:, columns(j)], out_sem.at[m])

    def deliver(m, out, j, slots):
        back = jnp.dot(unpick[m], slots.reshape(count, cw), preferred_element_type=f32)
        out_buf[m, j] = back.astype(bf16)
        out_copy(m, out, j).start()

    def finish_bwd(j):
        own_copy(BWD, j).wait_recv()
        for way, here, there in ((0, chip_a, across_a), (1, chip_b, across_b)):
            side_copy(j, way, plane, plane, here).wait_recv()
            side_copy(j, way, other, other, there).wait_recv()
        sums[plane] = part_bwd[j, y, plane]
        sums[other] = own_recv[BWD, j].astype(f32)
        value = sums[...] + side_recv[0, j].astype(f32) + side_recv[1, j].astype(f32)
        deliver(BWD, grad_in, j, value.astype(bf16))

    def finish_fwd(j):
        own_copy(FWD, j).wait_recv()
        pair_copy(j, plane, plane, chip_a).wait_recv()
        pair_copy(j, other, other, across_a).wait_recv()
        sums[plane] = part_fwd[j, side, plane]
        sums[other] = own_recv[FWD, j].astype(f32)
        value = (sums[...] + pair_recv[j].astype(f32)).reshape(count, cw) * factor[FWD][:, 0:1]
        deliver(FWD, result, j, (disp[FWD, j].astype(f32).reshape(count, cw) + value).astype(bf16))

    def at_step(i, start, action):
        j = i - start

        @pl.when((j >= 0) & (j < CHUNKS))
        def _():
            action(j)

    relay_bwd(0)

    def step(i, carry):
        at_step(i, -1, relay_bwd)
        at_step(i, RELAY_AT, relay_fwd)
        at_step(i, TWIN_AT, down_twin)
        at_step(i, 0, dispatch_bwd)
        at_step(i, FWD_AT, dispatch_fwd)
        at_step(i, SPREAD, spread_bwd)
        at_step(i, FWD_AT + SPREAD, spread_fwd)
        at_step(i, FWD_AT + FORWARD, forward_fwd)
        at_step(i, BWD_MULTIPLY_AT, multiply_bwd)
        at_step(i, FWD_MULTIPLY_AT, multiply_fwd)
        pl.when(i == BWD_INNER_AT)(finish_inner_grad)
        at_step(i, BWD_SUM_AT[0], produce_bwd)
        at_step(i, BWD_SUM_AT[1], add_bwd)
        at_step(i, BWD_SUM_AT[2], send_side)
        at_step(i, FWD_SUM_AT[0], produce_fwd)
        at_step(i, FWD_SUM_AT[1], finish_fwd)
        at_step(i, BWD_SUM_AT[3], finish_bwd)
        return carry

    lax.fori_loop(0, max(BWD_SUM_AT[3], FWD_SUM_AT[1]) + CHUNKS, step, 0)

    for one in shares:
        one.wait_send()
    grad_swap().wait_send()
    inner_swap().wait_send()

    def sent(ref, sem):
        pltpu.make_async_copy(ref, ref, sem).wait()

    sent(arr.at[0:2], pp_send)
    pl.when(on_edge)(lambda: sent(arr.at[0], relay_send))
    sent(down.at[:, 0], down_send)
    sent(down.at[:, 0], down_core_send)
    narrow = disp.at[0, :, 0]
    for m in range(2):
        sent(narrow, x_send.at[m])
        sent(narrow, bwd_send.at[m])
        sent(narrow, own_send_sem.at[m])
        sent(out_buf.at[m], out_sem.at[m])
        sent(side_send.at[m], side_send_sem.at[m])
    for at in range(4):
        sent(narrow, fwd_send.at[at])
    sent(pair_send, fwd_send.at[4])
    sent(pair_send, pair_send_sem)
    sent(far_send, far_send_sem)


def local(
    section_out,
    routes_fwd,
    gates_fwd,
    cot_next,
    routes_bwd,
    gates_bwd,
    norm_gain,
    saved_gate,
    saved_up,
    w_gate,
    w_up,
    w_down,
):
    count, width = section_out.shape
    cap = count // EXPERTS
    unit = w_gate.shape[2]
    units = unit * CORES
    total = RING * count
    cw = width // CHUNKS
    held = (EXPERTS, RING, CORES, cap, unit)
    f32, bf16 = jnp.float32, jnp.bfloat16
    vmem = pl.BlockSpec(memory_space=pltpu.VMEM)
    hbm = pl.BlockSpec(memory_space=pl.ANY)
    dma = pltpu.SemaphoreType.DMA
    block = (EXPERTS, cap, cw)
    first, second = pl.pallas_call(
        kernel,
        out_shape=[jax.ShapeDtypeStruct((count, width), bf16)] * 2,
        in_specs=[hbm, hbm, vmem, vmem, vmem, vmem, vmem] + [hbm] * 5,
        out_specs=[hbm, hbm],
        scratch_shapes=[
            pltpu.VMEM((2, CHUNKS, count, cw), bf16),
            pltpu.VMEM((3, CHUNKS, count, cw), bf16),
            pltpu.VMEM((2, CHUNKS) + block, bf16),
            pltpu.VMEM((CHUNKS, RING) + block, bf16),
            pltpu.VMEM((CHUNKS, 2) + block, bf16),
            pltpu.VMEM((2 * CORES, width, unit), bf16),
            pltpu.VMEM((CHUNKS, 2 * CORES, unit, cw), bf16),
            pltpu.VMEM((CORES, RING, EXPERTS, cap, unit), bf16),
            pltpu.VMEM((CORES, RING, EXPERTS, cap, unit), bf16),
            pltpu.VMEM((2, count, count), bf16),
            pltpu.VMEM((2, count, count), bf16),
            pltpu.VMEM((2, count, 128), f32),
            pltpu.VMEM((total, 2 * units), f32),
            pltpu.VMEM((total, 128), f32),
            pltpu.VMEM((2, count, units), bf16),
            pltpu.VMEM((2, count, 2 * units), bf16),
            pltpu.VMEM((2 * count, 2 * units), f32),
            pltpu.VMEM((2, count, units), bf16),
            pltpu.VMEM((2, count, units), bf16),
            pltpu.VMEM((RING, count, units), f32),
            pltpu.VMEM((total, 2 * units), bf16),
            pltpu.VMEM((CHUNKS, 2) + block, f32),
            pltpu.VMEM((CHUNKS, RING) + block, f32),
            pltpu.VMEM((CHUNKS,) + block, bf16),
            pltpu.VMEM((CHUNKS,) + block, bf16),
            pltpu.VMEM((CHUNKS,) + block, bf16),
            pltpu.VMEM((CHUNKS,) + block, bf16),
            pltpu.VMEM((2, CHUNKS) + block, bf16),
            pltpu.VMEM((2, CHUNKS) + block, bf16),
            pltpu.VMEM((2, CHUNKS, cap, cw), bf16),
            pltpu.VMEM((2, CHUNKS, cap, cw), bf16),
            pltpu.VMEM(block, f32),
            pltpu.VMEM((2, CHUNKS, count, cw), bf16),
            dma((2,)),
            dma((7,)),
            dma((7,)),
            dma((7,)),
            dma,
            dma((3, CHUNKS)),
            dma,
            dma((2,)),
            dma((2, CHUNKS)),
            dma((5,)),
            dma((CHUNKS, 6)),
            dma((2,)),
            dma((CHUNKS, 2)),
            dma,
            dma((CHUNKS,)),
            dma,
            dma((CHUNKS,)),
            dma((2,)),
            dma((2,)),
            dma,
            dma((CHUNKS, EXPERTS)),
            dma,
            dma((CHUNKS,)),
            dma((2,)),
            dma((2, CHUNKS, EXPERTS)),
            dma((2,)),
            dma((2, CHUNKS)),
            dma((2,)),
            pltpu.SemaphoreType.REGULAR((2,)),
        ],
        compiler_params=pltpu.CompilerParams(
            collective_id=0, has_side_effects=True, vmem_limit_bytes=58 * 1024 * 1024
        ),
        cost_estimate=pl.CostEstimate(
            flops=12 * total * width * units, bytes_accessed=16 * 1024 * 1024, transcendentals=2 * total * units
        ),
        name="relay_step",
    )(
        section_out,
        cot_next,
        routes_fwd.reshape(1, count),
        gates_fwd.reshape(1, count),
        routes_bwd.reshape(1, count),
        gates_bwd.reshape(1, count),
        norm_gain,
        saved_gate.reshape(held),
        saved_up.reshape(held),
        w_gate,
        w_up,
        w_down,
    )

    pieces = 4

    def settle(first, second, result, grad_in, held, sem):
        parts = []
        for m, (src, dst) in enumerate(((first, result), (second, grad_in))):
            for at in range(pieces):
                rows = pl.ds(at * (count // pieces), count // pieces)
                parts.append(
                    (
                        pltpu.make_async_copy(src.at[rows], held.at[m, rows], sem.at[0, m, at]),
                        pltpu.make_async_copy(held.at[m, rows], dst.at[rows], sem.at[1, m, at]),
                    )
                )
        for come, _ in parts:
            come.start()
        for come, go in parts:
            come.wait()
            go.start()
        for _, go in parts:
            go.wait()

    return pl.pallas_call(
        settle,
        out_shape=[jax.ShapeDtypeStruct((count, width), bf16)] * 2,
        in_specs=[hbm, hbm],
        out_specs=[hbm, hbm],
        scratch_shapes=[pltpu.VMEM((2, count, width), bf16), dma((2, 2, pieces))],
        compiler_params=pltpu.CompilerParams(vmem_limit_bytes=58 * 1024 * 1024),
        name="settle",
    )(first, second)


def solution(mesh):
    in_specs = (
        P(("pp", "ep"), None),
        P(("pp", "ep"), None),
        P(("pp", "ep"), None),
        P(("pp", "ep"), None),
        P(("pp", "ep"), None),
        P(("pp", "ep"), None),
        P("pp", None),
        P("pp", None, "ep"),
        P("pp", None, "ep"),
        P("pp", None, "ep"),
        P("pp", None, "ep"),
        P("pp", "ep", None),
    )
    out_specs = (P(("pp", "ep"), None), P(("pp", "ep"), None))

    def whole(*args):
        first, second = jax.shard_map(
            local, mesh=mesh, in_specs=in_specs, out_specs=out_specs, check_vma=False
        )(*args)
        return first, second

    return whole
```

```python
import jax
import jax.numpy as jnp
from jax import lax
from jax.experimental import pallas as pl
from jax.experimental.pallas import tpu as pltpu
from jax.sharding import PartitionSpec as P

EXPERTS = 2
RING = 4
CORES = 2
LAYERS = 16
EPS = 1e-06
CHUNKS = 4
MESH = pl.DeviceIdType.MESH
RELAY_AT = 1
TWIN_AT = 1
FWD_AT = 2
SPREAD = 1
FORWARD = 2
BWD_MULTIPLY_AT = 2
FWD_MULTIPLY_AT = 5
BWD_INNER_AT = 6
BWD_SUM_AT = (6, 8, 8, 11)
FWD_SUM_AT = (9, 11)
FWD, BWD, RELAY = 0, 1, 2


def kernel(
    section_out,
    cot_next,
    routes_fwd,
    gates_fwd,
    routes_bwd,
    gates_bwd,
    norm_gain,
    saved_gate,
    saved_up,
    w_gate,
    w_up,
    w_down,
    result,
    grad_in,
    leaving,
    arr,
    disp,
    rows_fwd,
    rows_bwd,
    gate_up,
    down,
    held_gate,
    held_up,
    pick,
    unpick,
    factor,
    act,
    squares,
    inner_send,
    inner,
    pair_grad,
    grad_send,
    grad_recv,
    inner_grad,
    both_grad,
    part_fwd,
    part_bwd,
    pair_send,
    pair_recv,
    far_send,
    far_recv,
    side_send,
    side_recv,
    own_send,
    own_recv,
    sums,
    out_buf,
    leaving_sem,
    load_sem,
    core_send,
    core_recv,
    pp_send,
    pp_recv,
    relay_send,
    x_send,
    x_recv,
    fwd_send,
    fwd_recv,
    bwd_send,
    bwd_recv,
    down_send,
    down_recv,
    down_core_send,
    down_core_recv,
    swap_send,
    swap_recv,
    pair_send_sem,
    pair_recv_sem,
    far_send_sem,
    far_recv_sem,
    side_send_sem,
    side_recv_sem,
    own_send_sem,
    own_recv_sem,
    out_sem,
    ready,
):
    count = section_out.shape[0]
    width = section_out.shape[1]
    cap = count // EXPERTS
    unit = w_gate.shape[2]
    units = unit * CORES
    cw = width // CHUNKS
    total = RING * count
    f32, bf16 = jnp.float32, jnp.bfloat16

    me_pp = lax.axis_index("pp")
    me = lax.axis_index("ep")
    n_pp = lax.axis_size("pp")
    layers = min(LAYERS, n_pp // 2)
    z = me_pp % layers
    z_base = me_pp - z
    wraps_up = (z + 1) // layers
    wraps_down = 1 - (z + layers - 1) // layers
    on_edge = (z == 0) | (z == layers - 1)
    split_way = z == 0
    plane = me // (RING * CORES)
    other = 1 - plane
    y = (me // CORES) % RING
    core = me % CORES
    half = y // 2
    side = y % 2
    y_a = y + 1 - 2 * side
    y_b = RING - 1 - y
    y_far = (y + 2) % RING

    def in_ring(at):
        return {"ep": plane * (RING * CORES) + at * CORES + core}

    chip_a = in_ring(y_a)
    chip_b = in_ring(y_b)
    across = {"ep": other * (RING * CORES) + y * CORES + core}
    across_a = {"ep": other * (RING * CORES) + y_a * CORES + core}
    across_b = {"ep": other * (RING * CORES) + y_b * CORES + core}
    twin = {"ep": plane * (RING * CORES) + y * CORES + (1 - core)}
    above = {"pp": z_base + (z + 1) % layers}
    below = {"pp": z_base + (z + layers - 1) % layers}
    mirror = {"pp": (me_pp + layers) % n_pp}

    barrier = pltpu.get_barrier_semaphore()

    def greet(**device):
        pl.semaphore_signal(barrier, inc=1, device_id=device, device_id_type=MESH)

    for at_plane, at_y in ((plane, y_a), (plane, y_b), (other, y), (other, y_a), (other, y_b)):
        greet(ep=at_plane * (RING * CORES) + at_y * CORES)
    pl.when(core == 1)(lambda: greet(ep=me - core))
    for section in (above, below, mirror):
        greet(pp=section["pp"], ep=me - core + 1)

    def tell(at):
        pl.semaphore_signal(ready.at[at], inc=1, device_id=twin, device_id_type=MESH)

    def columns(j):
        return pl.ds(pl.multiple_of(j * cw, cw), cw)

    def load_down(j):
        return pltpu.make_async_copy(w_down.at[0, :, columns(j)], down.at[j, core], load_sem.at[2])

    def load_rows(src, m, j):
        return pltpu.make_async_copy(src.at[:, columns(j)], leaving.at[m, j], leaving_sem.at[m])

    def start_loads(j, carry):
        load_rows(cot_next, BWD, j).start()
        load_rows(section_out, FWD, j).start()
        load_down(j).start()
        return carry

    lax.fori_loop(0, CHUNKS, start_loads, 0)
    loads = {}
    for at, (src, dst) in enumerate(
        [
            (w_gate.at[0], gate_up.at[core]),
            (w_up.at[0], gate_up.at[CORES + core]),
            (down.at[:, core], down.at[:, core]),
            (saved_gate.at[0, :, core], held_gate.at[core, :, 0]),
            (saved_gate.at[1, :, core], held_gate.at[core, :, 1]),
            (saved_up.at[0, :, core], held_up.at[core, :, 0]),
            (saved_up.at[1, :, core], held_up.at[core, :, 1]),
        ]
    ):
        loads[at] = pltpu.make_async_copy(src, dst, load_sem.at[at])
    for at in (0, 1, 3, 4, 5, 6):
        loads[at].start()
    @pl.when(core == 0)
    def _():
        pl.semaphore_wait(barrier, 5 * CORES + 1)
        tell(0)

    @pl.when(core == 1)
    def _():
        pl.semaphore_wait(ready.at[0], 1)

    loads[2].wait()

    def remote(src, dst, send, recv, to):
        return pltpu.make_async_remote_copy(
            src_ref=src, dst_ref=dst, send_sem=send, recv_sem=recv, device_id=to, device_id_type=MESH
        )

    def pp_copy(m, at, j, to):
        return remote(leaving.at[m, j], arr.at[at, j], pp_send, pp_recv.at[at, j], to)

    def down_copy(j):
        return remote(down.at[j, core], down.at[j, CORES + core], down_send, down_recv.at[j], chip_b)

    def start_down(j, carry):
        down_copy(j).start()
        return carry

    lax.fori_loop(0, CHUNKS, start_down, 0)

    def shared(src, dst, at):
        return remote(src, dst, core_send.at[at], core_recv.at[at], twin)

    shares = [
        shared(gate_up.at[core], gate_up.at[core], 0),
        shared(gate_up.at[CORES + core], gate_up.at[CORES + core], 1),
        shared(down.at[:, core], down.at[:, core], 2),
        shared(saved_gate.at[0, :, 1 - core], held_gate.at[core, :, 0], 3),
        shared(saved_gate.at[1, :, 1 - core], held_gate.at[core, :, 1], 4),
        shared(saved_up.at[0, :, 1 - core], held_up.at[core, :, 0], 5),
        shared(saved_up.at[1, :, 1 - core], held_up.at[core, :, 1], 6),
    ]
    for at in (2, 0, 1, 3, 4, 5, 6):
        if at < 2:
            loads[at].wait()
        shares[at].start()

    @pl.when(core == 1)
    def _():
        pl.semaphore_wait(barrier, 3 * CORES)
        tell(1)

    @pl.when(core == 0)
    def _():
        pl.semaphore_wait(ready.at[1], 1)

    for m in (BWD, FWD):
        pltpu.make_async_copy(leaving.at[m], leaving.at[m], leaving_sem.at[m]).wait()

    def start_first(j, carry):
        pp_copy(BWD, BWD + wraps_down, j, below).start()
        pp_copy(FWD, FWD + 2 * wraps_up, j, above).start()
        return carry

    lax.fori_loop(0, CHUNKS, start_first, 0)

    first = lax.broadcasted_iota(jnp.int32, (count, count), 0)
    second = lax.broadcasted_iota(jnp.int32, (count, count), 1)
    diagonal = first == second
    ones = jnp.ones((count, count), bf16)

    def places(routes, m):
        along = jnp.broadcast_to(routes[...].astype(f32), (count, count))
        down_rows = jnp.dot(jnp.where(diagonal, along, 0.0).astype(bf16), ones, preferred_element_type=f32)
        same = along == down_rows
        earlier = jnp.where(same & (first < second), 1.0, 0.0)
        place_along = along * cap + jnp.sum(earlier, axis=0, keepdims=True)
        chosen = place_along == first.astype(f32)
        pick[m] = jnp.where(chosen, 1.0, 0.0).astype(bf16)
        earlier = jnp.where(same & (second < first), 1.0, 0.0)
        place_down = down_rows * cap + jnp.sum(earlier, axis=1, keepdims=True)
        unpick[m] = jnp.where(place_down == second.astype(f32), 1.0, 0.0).astype(bf16)
        return chosen

    for m, routes, gates in ((BWD, routes_bwd, gates_bwd), (FWD, routes_fwd, gates_fwd)):
        chosen = places(routes, m)
        along = jnp.broadcast_to(gates[...], (count, count))
        slot_gate = jnp.sum(jnp.where(chosen, along, 0.0), axis=1, keepdims=True)
        factor[m] = jnp.broadcast_to(slot_gate, (count, 128))
    squares[...] = jnp.zeros_like(squares)
    act[...] = jnp.zeros_like(act)
    pair_grad[...] = jnp.zeros_like(pair_grad)

    def relay(j, m):
        pp_copy(FWD, RELAY, j, above).wait_recv()
        remote(arr.at[RELAY, j], arr.at[m, j], relay_send, pp_recv.at[m, j], mirror).start()

    def relay_fwd(j):
        pl.when(z == 0)(lambda: relay(j, FWD))

    def relay_bwd(j):
        pl.when(z == layers - 1)(lambda: relay(j, BWD))

    def down_twin(j):
        down_copy(j).wait_recv()
        mine = down.at[j, CORES + core]
        remote(mine, mine, down_core_send, down_core_recv.at[j], twin).start()

    def cross(m, rows, at, j, sender):
        return remote(disp.at[m, j, other], rows.at[j, at, sender], x_send.at[m], x_recv.at[m, j], across)

    def bwd_copy(j, expert):
        mine = rows_bwd.at[j, side, expert]
        return remote(mine, mine, bwd_send.at[expert], bwd_recv.at[j, expert], chip_a)

    def bwd_arrival(j, expert):
        theirs = rows_bwd.at[j, 1 - side, expert]
        return remote(theirs, theirs, bwd_send.at[expert], bwd_recv.at[j, expert], chip_a)

    def dispatch_bwd(j):
        pp_copy(BWD, BWD, j, below).wait_recv()
        moved = jnp.dot(pick[BWD], arr[BWD, j], preferred_element_type=f32) * factor[BWD][:, 0:1]
        disp[BWD, j] = moved.astype(bf16).reshape(EXPERTS, cap, cw)
        cross(BWD, rows_bwd, side, j, plane).start()
        rows_bwd[j, side, plane] = disp[BWD, j, plane]
        bwd_copy(j, plane).start()

    def spread_bwd(j):
        cross(BWD, rows_bwd, side, j, other).wait_recv()
        bwd_copy(j, other).start()

    def fwd_copy(j, at, expert, to, sem):
        mine = rows_fwd.at[j, at, expert]
        return remote(mine, mine, fwd_send.at[sem], fwd_recv.at[j, sem], to)

    def pass_copy(j, at, expert, to):
        block = rows_fwd.at[j, at, expert]
        return remote(block, block, fwd_send.at[4], fwd_recv.at[j, 4 + expert], to)

    def dispatch_fwd(j):
        pp_copy(FWD, FWD, j, above).wait_recv()
        moved = jnp.dot(pick[FWD], arr[FWD, j], preferred_element_type=f32)
        disp[FWD, j] = moved.astype(bf16).reshape(EXPERTS, cap, cw)
        cross(FWD, rows_fwd, y, j, plane).start()
        rows_fwd[j, y, plane] = disp[FWD, j, plane]
        fwd_copy(j, y, plane, chip_b, 2 + plane).start()
        fwd_copy(j, y, plane, chip_a, plane).start()

    def spread_fwd(j):
        cross(FWD, rows_fwd, y, j, other).wait_recv()
        fwd_copy(j, y, other, chip_b, 2 + other).start()
        fwd_copy(j, y, other, chip_a, other).start()

    def forward_fwd(j):
        fwd_copy(j, y_b, 0, chip_b, 2).wait_recv()
        pass_copy(j, y_b, 0, chip_a).start()

        @pl.when(split_way)
        def _():
            fwd_copy(j, y_a, 1, chip_a, 1).wait_recv()
            pass_copy(j, y_a, 1, chip_b).start()

        @pl.when(jnp.logical_not(split_way))
        def _():
            fwd_copy(j, y_b, 1, chip_b, 3).wait_recv()
            pass_copy(j, y_b, 1, chip_a).start()

    def wait_loads(which):
        for at in which:
            if at > 2:
                loads[at].wait()
            shares[at].wait_recv()

    def both_weights(j):
        return jnp.concatenate([gate_up[at, columns(j), :] for at in range(2 * CORES)], axis=1)

    def all_units(held):
        return jnp.concatenate([held[at].reshape(total, unit) for at in range(CORES)], axis=1).astype(f32)

    def grad_swap():
        return remote(grad_send, grad_recv, swap_send.at[BWD], swap_recv.at[BWD], chip_b)

    def inner_swap():
        return remote(
            inner_send, inner.at[:, :, units : 2 * units], swap_send.at[FWD], swap_recv.at[FWD], chip_b
        )

    def multiply_bwd(j):
        @pl.when(j == 0)
        def _():
            wait_loads((2,))

        for expert in range(EXPERTS):
            bwd_arrival(j, expert).wait_recv()
        theirs = down.at[j, CORES + 1 - core]
        remote(theirs, theirs, down_core_send, down_core_recv.at[j], twin).wait_recv()
        pair_grad[...] += lax.dot_general(
            rows_bwd[j].reshape(2 * count, cw),
            down[j].reshape(2 * units, cw),
            (((1,), (1,)), ((), ())),
            preferred_element_type=f32,
        )

        @pl.when(j == CHUNKS - 1)
        def _():
            grad_send[...] = pair_grad[:, units : 2 * units].astype(bf16).reshape(2, count, units)
            grad_swap().start()
            inner_grad[pl.ds(2 * half, 2)] = pair_grad[:, 0:units].reshape(2, count, units)

    def finish_inner_grad():
        wait_loads((3, 4, 5, 6))
        grad_swap().wait_recv()
        inner_grad[pl.ds(2 * (1 - half), 2)] = grad_recv[...].astype(f32)
        grad = inner_grad[...].reshape(total, units)
        gate_act = all_units(held_gate)
        up_act = all_units(held_up)
        sigma = jax.nn.sigmoid(gate_act)
        both_grad[:, 0:units] = (grad * up_act * sigma * (1.0 + gate_act * (1.0 - sigma))).astype(bf16)
        both_grad[:, units : 2 * units] = (grad * gate_act * sigma).astype(bf16)

    def multiply_fwd(j):
        @pl.when(j == 0)
        def _():
            wait_loads((0, 1))

        fwd_copy(j, y_a, 0, chip_a, 0).wait_recv()

        @pl.when(split_way)
        def _():
            fwd_copy(j, y_b, 1, chip_b, 3).wait_recv()

        @pl.when(jnp.logical_not(split_way))
        def _():
            fwd_copy(j, y_a, 1, chip_a, 1).wait_recv()

        for expert in range(EXPERTS):
            pass_copy(j, y_far, expert, chip_a).wait_recv()
        floats = rows_fwd[j].reshape(total, cw).astype(f32)
        squared = floats * floats
        summed = squared[:, 0:128]
        for k in range(1, cw // 128):
            summed = summed + squared[:, k * 128 : (k + 1) * 128]
        squares[...] += summed
        left = (floats * norm_gain[:, columns(j)]).astype(bf16)
        act[...] += jnp.dot(left, both_weights(j), preferred_element_type=f32)

        @pl.when(j == CHUNKS - 1)
        def _():
            mean = jnp.sum(squares[...], axis=1, keepdims=True) * (1.0 / width)
            scale = lax.rsqrt(mean + EPS)
            gate_act = act[:, 0:units] * scale
            up_act = act[:, units : 2 * units] * scale
            value = (gate_act * jax.nn.sigmoid(gate_act) * up_act).astype(bf16).reshape(2, 2, count, units)
            for at in range(2):
                @pl.when(half == at)
                def _():
                    inner[:, :, 0:units] = value[at]
                    inner_send[...] = value[1 - at]
            inner_swap().start()

    def far_copy(j):
        return remote(far_send.at[j], far_recv.at[j], far_send_sem, far_recv_sem.at[j], chip_b)

    def side_copy(j, way, expert, sender, to):
        return remote(
            side_send.at[way, j, expert],
            side_recv.at[way, j, sender],
            side_send_sem.at[way],
            side_recv_sem.at[way, j, sender],
            to,
        )

    def own_copy(m, j):
        return remote(own_send.at[m, j], own_recv.at[m, j], own_send_sem.at[m], own_recv_sem.at[m, j], across)

    def produce_bwd(j):
        value = lax.dot_general(
            both_grad[...], both_weights(j), (((1,), (1,)), ((), ())), preferred_element_type=f32
        )
        part_bwd[j] = value.reshape(RING, EXPERTS, cap, cw)
        far_send[j] = part_bwd[j, y_far].astype(bf16)
        far_copy(j).start()
        own_send[BWD, j] = part_bwd[j, y, other].astype(bf16)
        own_copy(BWD, j).start()
        side_send[1, j] = part_bwd[j, y_b].astype(bf16)

    def send_side(j):
        side_copy(j, 1, plane, plane, chip_b).start()
        side_copy(j, 1, other, plane, across_b).start()

    def add_bwd(j):
        far_copy(j).wait_recv()
        side_send[0, j] = (part_bwd[j, y_a] + far_recv[j].astype(f32)).astype(bf16)
        side_copy(j, 0, plane, plane, chip_a).start()
        side_copy(j, 0, other, plane, across_a).start()

    def pair_copy(j, expert, sender, to):
        return remote(pair_send.at[j, expert], pair_recv.at[j, sender], pair_send_sem, pair_recv_sem.at[j, sender], to)

    def produce_fwd(j):
        @pl.when(j == 0)
        def _():
            inner_swap().wait_recv()

        value = jnp.dot(
            inner[...].reshape(2 * count, 2 * units), down[j].reshape(2 * units, cw), preferred_element_type=f32
        )
        part_fwd[j] = value.reshape(2, EXPERTS, cap, cw)
        pair_send[j] = part_fwd[j, 1 - side].astype(bf16)
        pair_copy(j, plane, plane, chip_a).start()
        pair_copy(j, other, plane, across_a).start()
        own_send[FWD, j] = part_fwd[j, side, other].astype(bf16)
        own_copy(FWD, j).start()

    def out_copy(m, out, j):
        return pltpu.make_async_copy(out_buf.at[m, j], out.at[:, columns(j)], out_sem.at[m])

    def deliver(m, out, j, slots):
        back = jnp.dot(unpick[m], slots.reshape(count, cw), preferred_element_type=f32)
        out_buf[m, j] = back.astype(bf16)
        out_copy(m, out, j).start()

    def finish_bwd(j):
        own_copy(BWD, j).wait_recv()
        for way, here, there in ((0, chip_a, across_a), (1, chip_b, across_b)):
            side_copy(j, way, plane, plane, here).wait_recv()
            side_copy(j, way, other, other, there).wait_recv()
        sums[plane] = part_bwd[j, y, plane]
        sums[other] = own_recv[BWD, j].astype(f32)
        value = sums[...] + side_recv[0, j].astype(f32) + side_recv[1, j].astype(f32)
        deliver(BWD, grad_in, j, value.astype(bf16))

    def finish_fwd(j):
        own_copy(FWD, j).wait_recv()
        pair_copy(j, plane, plane, chip_a).wait_recv()
        pair_copy(j, other, other, across_a).wait_recv()
        sums[plane] = part_fwd[j, side, plane]
        sums[other] = own_recv[FWD, j].astype(f32)
        value = (sums[...] + pair_recv[j].astype(f32)).reshape(count, cw) * factor[FWD][:, 0:1]
        deliver(FWD, result, j, (disp[FWD, j].astype(f32).reshape(count, cw) + value).astype(bf16))

    def at_step(i, start, action):
        j = i - start

        @pl.when((j >= 0) & (j < CHUNKS))
        def _():
            action(j)

    relay_bwd(0)

    def step(i, carry):
        at_step(i, -1, relay_bwd)
        at_step(i, RELAY_AT, relay_fwd)
        at_step(i, 0, dispatch_bwd)
        at_step(i, FWD_AT, dispatch_fwd)
        at_step(i, SPREAD, spread_bwd)
        at_step(i, FWD_AT + SPREAD, spread_fwd)
        at_step(i, FWD_AT + FORWARD, forward_fwd)
        at_step(i, TWIN_AT, down_twin)
        at_step(i, BWD_MULTIPLY_AT, multiply_bwd)
        at_step(i, FWD_MULTIPLY_AT, multiply_fwd)
        pl.when(i == BWD_INNER_AT)(finish_inner_grad)
        at_step(i, BWD_SUM_AT[0], produce_bwd)
        at_step(i, BWD_SUM_AT[1], add_bwd)
        at_step(i, BWD_SUM_AT[2], send_side)
        at_step(i, FWD_SUM_AT[0], produce_fwd)
        at_step(i, FWD_SUM_AT[1], finish_fwd)
        at_step(i, BWD_SUM_AT[3], finish_bwd)
        return carry

    lax.fori_loop(0, max(BWD_SUM_AT[3], FWD_SUM_AT[1]) + CHUNKS, step, 0)

    for one in shares:
        one.wait_send()
    grad_swap().wait_send()
    inner_swap().wait_send()

    def sent(ref, sem):
        pltpu.make_async_copy(ref, ref, sem).wait()

    sent(arr.at[0:2], pp_send)
    pl.when(on_edge)(lambda: sent(arr.at[0], relay_send))
    sent(down.at[:, 0], down_send)
    sent(down.at[:, 0], down_core_send)
    narrow = disp.at[0, :, 0]
    for m in range(2):
        sent(narrow, x_send.at[m])
        sent(narrow, bwd_send.at[m])
        sent(narrow, own_send_sem.at[m])
        sent(out_buf.at[m], out_sem.at[m])
        sent(side_send.at[m], side_send_sem.at[m])
    for at in range(4):
        sent(narrow, fwd_send.at[at])
    sent(pair_send, fwd_send.at[4])
    sent(pair_send, pair_send_sem)
    sent(far_send, far_send_sem)


def local(
    section_out,
    routes_fwd,
    gates_fwd,
    cot_next,
    routes_bwd,
    gates_bwd,
    norm_gain,
    saved_gate,
    saved_up,
    w_gate,
    w_up,
    w_down,
):
    count, width = section_out.shape
    cap = count // EXPERTS
    unit = w_gate.shape[2]
    units = unit * CORES
    total = RING * count
    cw = width // CHUNKS
    held = (EXPERTS, RING, CORES, cap, unit)
    f32, bf16 = jnp.float32, jnp.bfloat16
    vmem = pl.BlockSpec(memory_space=pltpu.VMEM)
    hbm = pl.BlockSpec(memory_space=pl.ANY)
    dma = pltpu.SemaphoreType.DMA
    block = (EXPERTS, cap, cw)
    first, second = pl.pallas_call(
        kernel,
        out_shape=[jax.ShapeDtypeStruct((count, width), bf16)] * 2,
        in_specs=[hbm, hbm, vmem, vmem, vmem, vmem, vmem] + [hbm] * 5,
        out_specs=[hbm, hbm],
        scratch_shapes=[
            pltpu.VMEM((2, CHUNKS, count, cw), bf16),
            pltpu.VMEM((3, CHUNKS, count, cw), bf16),
            pltpu.VMEM((2, CHUNKS) + block, bf16),
            pltpu.VMEM((CHUNKS, RING) + block, bf16),
            pltpu.VMEM((CHUNKS, 2) + block, bf16),
            pltpu.VMEM((2 * CORES, width, unit), bf16),
            pltpu.VMEM((CHUNKS, 2 * CORES, unit, cw), bf16),
            pltpu.VMEM((CORES, RING, EXPERTS, cap, unit), bf16),
            pltpu.VMEM((CORES, RING, EXPERTS, cap, unit), bf16),
            pltpu.VMEM((2, count, count), bf16),
            pltpu.VMEM((2, count, count), bf16),
            pltpu.VMEM((2, count, 128), f32),
            pltpu.VMEM((total, 2 * units), f32),
            pltpu.VMEM((total, 128), f32),
            pltpu.VMEM((2, count, units), bf16),
            pltpu.VMEM((2, count, 2 * units), bf16),
            pltpu.VMEM((2 * count, 2 * units), f32),
            pltpu.VMEM((2, count, units), bf16),
            pltpu.VMEM((2, count, units), bf16),
            pltpu.VMEM((RING, count, units), f32),
            pltpu.VMEM((total, 2 * units), bf16),
            pltpu.VMEM((CHUNKS, 2) + block, f32),
            pltpu.VMEM((CHUNKS, RING) + block, f32),
            pltpu.VMEM((CHUNKS,) + block, bf16),
            pltpu.VMEM((CHUNKS,) + block, bf16),
            pltpu.VMEM((CHUNKS,) + block, bf16),
            pltpu.VMEM((CHUNKS,) + block, bf16),
            pltpu.VMEM((2, CHUNKS) + block, bf16),
            pltpu.VMEM((2, CHUNKS) + block, bf16),
            pltpu.VMEM((2, CHUNKS, cap, cw), bf16),
            pltpu.VMEM((2, CHUNKS, cap, cw), bf16),
            pltpu.VMEM(block, f32),
            pltpu.VMEM((2, CHUNKS, count, cw), bf16),
            dma((2,)),
            dma((7,)),
            dma((7,)),
            dma((7,)),
            dma,
            dma((3, CHUNKS)),
            dma,
            dma((2,)),
            dma((2, CHUNKS)),
            dma((5,)),
            dma((CHUNKS, 6)),
            dma((2,)),
            dma((CHUNKS, 2)),
            dma,
            dma((CHUNKS,)),
            dma,
            dma((CHUNKS,)),
            dma((2,)),
            dma((2,)),
            dma,
            dma((CHUNKS, EXPERTS)),
            dma,
            dma((CHUNKS,)),
            dma((2,)),
            dma((2, CHUNKS, EXPERTS)),
            dma((2,)),
            dma((2, CHUNKS)),
            dma((2,)),
            pltpu.SemaphoreType.REGULAR((2,)),
        ],
        compiler_params=pltpu.CompilerParams(
            collective_id=0, has_side_effects=True, vmem_limit_bytes=58 * 1024 * 1024
        ),
        cost_estimate=pl.CostEstimate(
            flops=12 * total * width * units, bytes_accessed=16 * 1024 * 1024, transcendentals=2 * total * units
        ),
        name="relay_step",
    )(
        section_out,
        cot_next,
        routes_fwd.reshape(1, count),
        gates_fwd.reshape(1, count),
        routes_bwd.reshape(1, count),
        gates_bwd.reshape(1, count),
        norm_gain,
        saved_gate.reshape(held),
        saved_up.reshape(held),
        w_gate,
        w_up,
        w_down,
    )

    pieces = 4

    def settle(first, second, result, grad_in, held, sem):
        parts = []
        for m, (src, dst) in enumerate(((first, result), (second, grad_in))):
            for at in range(pieces):
                rows = pl.ds(at * (count // pieces), count // pieces)
                parts.append(
                    (
                        pltpu.make_async_copy(src.at[rows], held.at[m, rows], sem.at[0, m, at]),
                        pltpu.make_async_copy(held.at[m, rows], dst.at[rows], sem.at[1, m, at]),
                    )
                )
        for come, _ in parts:
            come.start()
        for come, go in parts:
            come.wait()
            go.start()
        for _, go in parts:
            go.wait()

    return pl.pallas_call(
        settle,
        out_shape=[jax.ShapeDtypeStruct((count, width), bf16)] * 2,
        in_specs=[hbm, hbm],
        out_specs=[hbm, hbm],
        scratch_shapes=[pltpu.VMEM((2, count, width), bf16), dma((2, 2, pieces))],
        compiler_params=pltpu.CompilerParams(vmem_limit_bytes=58 * 1024 * 1024),
        name="settle",
    )(first, second)


def solution(mesh):
    in_specs = (
        P(("pp", "ep"), None),
        P(("pp", "ep"), None),
        P(("pp", "ep"), None),
        P(("pp", "ep"), None),
        P(("pp", "ep"), None),
        P(("pp", "ep"), None),
        P("pp", None),
        P("pp", None, "ep"),
        P("pp", None, "ep"),
        P("pp", None, "ep"),
        P("pp", None, "ep"),
        P("pp", "ep", None),
    )
    out_specs = (P(("pp", "ep"), None), P(("pp", "ep"), None))

    def whole(*args):
        first, second = jax.shard_map(
            local, mesh=mesh, in_specs=in_specs, out_specs=out_specs, check_vma=False
        )(*args)
        return first, second

    return whole
```
